256 devices in a mesh: depth: 16 (over x, y), row: 2 (over z_hi), col: 8 (over z_lo, core).
Axes of the slice: x: 4, y: 4, z: 8 (z_hi: 2, z_lo: 4; z = z_hi * 4 + z_lo), core: 2. Of those that a mesh axis runs over, the one named last changes fastest.
Arguments:
- inputs: bfloat16 [4608, 4096], P('depth', ('row', 'col')), may hold values from -6 to 6
- gate_weight: bfloat16 [2, 2048, 14336], P('row', 'depth', 'col'), may hold values from -0.09375 to 0.09375
- up_weight: bfloat16 [2, 2048, 14336], P('row', 'depth', 'col'), may hold values from -0.09375 to 0.09375
- cotangent: bfloat16 [4608, 14336], P(('depth', 'row'), 'col'), may hold values from -1.5 to 1.5
Outputs:
- hidden: bfloat16 [4608, 14336], P(('depth', 'row'), 'col')
- input_grad: bfloat16 [4608, 4096], P('depth', ('row', 'col'))
- gate_grad: bfloat16 [2, 2048, 14336], P('row', 'depth', 'col')
- up_grad: bfloat16 [2, 2048, 14336], P('row', 'depth', 'col')
The draws below stay inside these ranges and needn't reach their ends.
All inputs are finite; a program needn't handle non-finite values.
Results may differ from the reference program's by a relative error of at most 0.024.
Values may be sent and summed in bfloat16 or wider, within the bound.
A program may use at most 128 MiB of HBM per device.

```python
import jax
import jax.numpy as jnp
from jax import lax

D = 4096
FF = 14336
TOK_DEV = 288
TOKENS = 4608
DB = 2048
N_DEPTH = 16
N_ROW = 2
N_COL = 8


def levels(own_key, shape, shards, low, high):
    def one(axis_at, blocks):
        heights = jax.random.uniform(jax.random.fold_in(jax.random.fold_in(own_key, 6), axis_at), (blocks,), jnp.float32, low / len(shards), high / len(shards))
        return jnp.repeat(jnp.exp(heights), shape[axis_at] // blocks).reshape((-1,) + (1,) * (len(shape) - axis_at - 1))

    factor_of = one(*shards[0])
    for cut in shards[1:]:
        factor_of = factor_of * one(*cut)
    return factor_of


def noise(rng, shape, spread, most, cuts=(), held_as=jnp.bfloat16):
    drawn = jax.random.normal(rng, shape, jnp.float32) * spread
    if len(cuts) > 0:
        drawn = levels(rng, shape, cuts, -0.22, 0.18) * drawn
    return jnp.clip(drawn, min=-most, max=most).astype(held_as)


def setup_inputs(seed: int = 0) -> dict:
    streams_of = jax.random.split(jax.random.key(seed), 5)
    inputs = noise(streams_of[0], (TOKENS, D), 1.0, 6.0, ((0, 16), (1, 16)))
    gate_weight = noise(streams_of[1], (N_ROW, DB, FF), D ** -0.5, 0.09375, ((0, 2), (1, 16), (2, 8)))
    up_weight = noise(streams_of[2], (N_ROW, DB, FF), D ** -0.5, 0.09375, ((0, 2), (1, 16), (2, 8)))
    cotangent = noise(streams_of[3], (TOKENS, FF), 0.25, 1.5, ((0, 32), (1, 8)))
    return dict(inputs=inputs, gate_weight=gate_weight, up_weight=up_weight, cotangent=cotangent)


def rounded(value):
    return lax.optimization_barrier(value.astype(jnp.bfloat16)).astype(jnp.float32)


def reference(inputs, gate_weight, up_weight, cotangent):
    block = D // N_ROW
    hid_block = FF // N_COL
    gate_full = gate_weight.reshape(D, FF)
    up_full = up_weight.reshape(D, FF)
    gate_sum = jnp.zeros((TOKENS, FF), jnp.float32)
    up_sum = jnp.zeros((TOKENS, FF), jnp.float32)
    for index in range(N_ROW):
        columns = inputs[:, index * block:(index + 1) * block]
        gate_sum = gate_sum + rounded(jnp.dot(columns, gate_full[index * block:(index + 1) * block], preferred_element_type=jnp.float32))
        up_sum = up_sum + rounded(jnp.dot(columns, up_full[index * block:(index + 1) * block], preferred_element_type=jnp.float32))
    sig = jax.nn.sigmoid(gate_sum)
    act = gate_sum * sig
    hidden = (act * up_sum).astype(jnp.bfloat16)
    upstream = cotangent.astype(jnp.float32)
    up_delta = (upstream * act).astype(jnp.bfloat16)
    gate_delta = (upstream * up_sum * sig * (1.0 + gate_sum * (1.0 - sig))).astype(jnp.bfloat16)
    dims = (((1,), (1,)), ((), ()))
    input_total = jnp.zeros((TOKENS, D), jnp.float32)
    for index in range(N_COL):
        lower = index * hid_block
        upper = lower + hid_block
        part = lax.dot_general(gate_delta[:, lower:upper], gate_full[:, lower:upper], dims, preferred_element_type=jnp.float32)
        part = part + lax.dot_general(up_delta[:, lower:upper], up_full[:, lower:upper], dims, preferred_element_type=jnp.float32)
        input_total = input_total + rounded(part)
    input_grad = input_total.astype(jnp.bfloat16)
    group_inputs = inputs.reshape(N_DEPTH, TOK_DEV, D)
    group_gate = gate_delta.reshape(N_DEPTH, TOK_DEV, FF)
    group_up = up_delta.reshape(N_DEPTH, TOK_DEV, FF)
    tdims = (((0,), (0,)), ((), ()))

    def accumulate(carry, group):
        rows, gate_rows, up_rows = group
        gate_acc = carry[0] + rounded(lax.dot_general(rows, gate_rows, tdims, preferred_element_type=jnp.float32))
        up_acc = carry[1] + rounded(lax.dot_general(rows, up_rows, tdims, preferred_element_type=jnp.float32))
        return (gate_acc, up_acc), None

    start = (jnp.zeros((D, FF), jnp.float32), jnp.zeros((D, FF), jnp.float32))
    totals, _ = lax.scan(accumulate, start, (group_inputs, group_gate, group_up))
    gate_grad = totals[0].astype(jnp.bfloat16).reshape(N_ROW, block, FF)
    up_grad = totals[1].astype(jnp.bfloat16).reshape(N_ROW, block, FF)
    return hidden, input_grad, gate_grad, up_grad
```

```python
import functools

import jax
import jax.numpy as jnp
from jax import lax
from jax.experimental import pallas as pl
from jax.experimental.pallas import tpu as pltpu
from jax.sharding import PartitionSpec as P

MESH = pl.DeviceIdType.MESH
BF = jnp.bfloat16
F32 = jnp.float32
NX = 4
ROWS = 128
CW = 128
TICKS_TO_FORWARD = 4


def kernel(
    nch, x_hbm, gw_hbm, uw_hbm, cot_hbm, hid_ref, dx_ref, gg_ref, ug_ref,
    panel, gpart, rb0, rb1, rb2, rb3, xp, xt, acc, part, zin, dl, cot, dxs, dxr, dxz, dxq,
    loc_sem, in_sem, ag_send, ag_recv, rs_send, rs_recv, z_send, z_recv, x_send, x_recv, d_send, d_recv,
):
    d, r, c = lax.axis_index("depth"), lax.axis_index("row"), lax.axis_index("col")
    x, y = lax.div(d, NX), lax.rem(d, NX)
    zl, k = lax.div(c, 2), lax.rem(c, 2)
    tok = dx_ref.shape[0]
    half = tok // 2
    fb = dx_ref.shape[1]

    def ring(p, s):
        return lax.rem(p + s + NX, NX)

    def x_dev(s):
        return {"depth": ring(x, s) * NX + y}

    def y_dev(s):
        return {"depth": x * NX + ring(y, s)}

    row_dev = {"row": 1 - r}
    sib_dev = {"col": c + 1 - 2 * k}

    def z_dev(s):
        return {"col": ring(zl, s) * 2 + k}

    def remote(src, dst, ssem, rsem, dev):
        return pltpu.make_async_remote_copy(
            src_ref=src, dst_ref=dst, send_sem=ssem, recv_sem=rsem, device_id=dev, device_id_type=MESH
        )

    def cols(j):
        return pl.ds(pl.multiple_of(j * CW, CW), CW)

    def feat(b):
        return pl.ds(pl.multiple_of(b * fb, fb), fb)

    w_hbm = (gw_hbm, uw_hbm)

    def own(j, s):
        return pltpu.make_async_copy(w_hbm[s].at[0, :, cols(j)], panel.at[j, s, x, y], loc_sem.at[s, j])

    own_x = pltpu.make_async_copy(x_hbm, xp.at[:, feat(c)], in_sem.at[0])
    own_cot = pltpu.make_async_copy(cot_hbm, cot, in_sem.at[1])

    def start_own(j, carry):
        for s in range(2):
            own(j, s).start()
        return carry

    own_x.start()
    lax.fori_loop(0, nch, start_own, 0)
    own_cot.start()

    partners = [x_dev(1), x_dev(-1), y_dev(1), y_dev(-1), row_dev, sib_dev, z_dev(1), z_dev(2), z_dev(3)]
    barrier = pltpu.get_barrier_semaphore()
    for dev in partners:
        pl.semaphore_signal(barrier, inc=1, device_id=dev, device_id_type=MESH)
    pl.semaphore_wait(barrier, len(partners))

    def x_line(s, b):
        blk = xp.at[:, feat(b)]
        return remote(blk, blk, x_send.at[s - 1], x_recv.at[s - 1], z_dev(s))

    def x_sib(s, b):
        blk = xp.at[:, feat(b)]
        return remote(blk, blk, x_send.at[3 + s], x_recv.at[3 + s], sib_dev)

    def x_start():
        own_x.wait()
        for s in (1, 2, 3):
            x_line(s, c).start()
        x_sib(0, c).start()

    def x_forward():
        for s in (1, 3, 2):
            b = ring(zl, -s) * 2 + k
            x_line(s, b).wait_recv()
            x_sib(s, b).start()

    def x_finish():
        for s in (1, 2, 3):
            x_line(s, c).wait_send()
        for s in range(4):
            b = ring(zl, -s) * 2 + 1 - k
            x_sib(s, b).wait_recv()
            x_sib(s, c).wait_send()
        for i in range(NX):
            w = 4 * ROWS
            xt[i] = jnp.transpose(xp[:, i * w : (i + 1) * w])

    def ring_dev(axis, s):
        return x_dev(s) if axis == 0 else y_dev(s)

    def me(axis):
        return x if axis == 0 else y

    def block(buf, j, s, p):
        return buf.at[j, 0, p, y] if s == 0 else buf.at[j, 1, x, p]

    def block_half(buf, j, s, p, h):
        rows = pl.ds(h * (ROWS // 2), ROWS // 2)
        return buf.at[j, 0, p, y, rows] if s == 0 else buf.at[j, 1, x, p, rows]

    def group(buf, j, s, q):
        return buf.at[j, 0, :, q] if s == 0 else buf.at[j, 1, q]

    def group_half(buf, j, s, q, h):
        return buf.at[j, 0, pl.ds(2 * h, 2), q] if s == 0 else buf.at[j, 1, q, pl.ds(2 * h, 2)]

    def ag(stage, j, s, i, src):
        axis = s if stage < 2 else 1 - s
        return remote(
            src, src, ag_send.at[stage, s, i, j], ag_recv.at[stage, s, i, j], ring_dev(axis, 1 - 2 * i)
        )

    def ag0(j):
        for s in range(2):
            own(j, s).wait()
        for s in range(2):
            for i in range(2):
                ag(0, j, s, i, block(panel, j, s, me(s))).start()

    def ag1(j):
        for s in range(2):
            m = me(s)
            for i in range(2):
                src = ring(m, -1 + 2 * i)
                ag(0, j, s, i, block(panel, j, s, src)).wait_recv()
                ag(1, j, s, i, block_half(panel, j, s, src, i)).start()
        for s in range(2):
            for i in range(2):
                ag(0, j, s, i, block(panel, j, s, me(s))).wait_send()

    def ag2(j):
        for s in range(2):
            m = me(s)
            for i in range(2):
                ag(1, j, s, i, block_half(panel, j, s, ring(m, 2), i)).wait_recv()
            for i in range(2):
                ag(2, j, s, i, group(panel, j, s, me(1 - s))).start()
        for s in range(2):
            for i in range(2):
                ag(1, j, s, i, block_half(panel, j, s, me(s), i)).wait_send()

    def ag3(j):
        for s in range(2):
            m = me(1 - s)
            for i in range(2):
                src = ring(m, -1 + 2 * i)
                ag(2, j, s, i, group(panel, j, s, src)).wait_recv()
                ag(3, j, s, i, group_half(panel, j, s, src, i)).start()
        for s in range(2):
            for i in range(2):
                ag(2, j, s, i, group(panel, j, s, me(1 - s))).wait_send()

    def ag4(j):
        for s in range(2):
            m = me(1 - s)
            for i in range(2):
                ag(3, j, s, i, group_half(panel, j, s, ring(m, 2), i)).wait_recv()
        for s in range(2):
            for i in range(2):
                ag(3, j, s, i, group_half(panel, j, s, me(1 - s), i)).wait_send()

    def z1(j, src):
        return remote(src, zin.at[j], z_send.at[0, j], z_recv.at[0, j], row_dev)

    def z2(j, h):
        return remote(dl.at[j, h], dl.at[j, h], z_send.at[1, j], z_recv.at[1, j], row_dev)

    def weights(j, i):
        n = 4 * ROWS
        return jnp.concatenate([panel[j, 0, i].reshape(n, CW), panel[j, 1, i].reshape(n, CW)], axis=1)

    def forward(j):
        ag4(j)
        w = jnp.concatenate([weights(j, i) for i in range(NX)], axis=0)
        out = jnp.dot(xp[...], w, preferred_element_type=F32)
        part[j] = out.reshape(2, half, 2 * CW).astype(BF)
        z1(j, part.at[j, 1 - r]).start()

    def deltas(j):
        z1(j, part.at[j, 1 - r]).wait()
        total = part[j, r].astype(F32) + zin[j].astype(F32)
        gate, up = total[:, :CW], total[:, CW:]
        sig = jax.nn.sigmoid(gate)
        act = gate * sig
        hid_ref[:, cols(j)] = (act * up).astype(BF)
        upstream = cot[:, cols(j)].astype(F32)
        gd = (upstream * up * sig * (1.0 + gate * (1.0 - sig))).astype(BF)
        ud = (upstream * act).astype(BF)
        dl[j, r] = jnp.concatenate([gd, ud], axis=1)
        z2(j, r).start()

    def grads(j):
        z2(j, 1 - r).wait_recv()
        z2(j, r).wait_send()

        def wgrad(i, carry):
            g = jnp.dot(xt[i], dl[j].reshape(tok, 2 * CW), preferred_element_type=F32).astype(BF)
            gpart[j, 0, i] = g[:, :CW].reshape(NX, ROWS, CW)
            gpart[j, 1, i] = g[:, CW:].reshape(NX, ROWS, CW)
            return carry

        lax.fori_loop(0, NX, wgrad, 0)
        rs0(j)

        def dgrad(i, carry):
            w = weights(j, i)
            p = lax.dot_general(
                dl[j].reshape(tok, 2 * CW), w, (((1,), (1,)), ((), ())), preferred_element_type=F32
            )
            sl = pl.ds(pl.multiple_of(i * 4 * ROWS, 4 * ROWS), 4 * ROWS)

            @pl.when(j == 0)
            def _():
                acc[:, sl] = p

            @pl.when(j > 0)
            def _():
                acc[:, sl] += p

            return carry

        lax.fori_loop(0, NX, dgrad, 0)

    def rs(stage, j, s, i, src):
        axis = 1 - s if stage < 2 else s
        dst = (rb0, rb1, rb2, rb3)[stage].at[j, s, i]
        return remote(src, dst, rs_send.at[stage, s, i, j], rs_recv.at[stage, s, i, j], ring_dev(axis, 1 - 2 * i))

    def add(ref, *others):
        v = ref[...].astype(F32)
        for o in others:
            v = v + o[...].astype(F32)
        ref[...] = v.astype(BF)

    def rs0(j):
        for s in range(2):
            far = ring(me(1 - s), 2)
            for i in range(2):
                rs(0, j, s, i, group_half(gpart, j, s, far, i)).start()

    def rs1(j):
        for s in range(2):
            m = me(1 - s)
            for i in range(2):
                rs(0, j, s, i, group_half(gpart, j, s, ring(m, 2), i)).wait_recv()
                near = ring(m, 1 - 2 * i)
                add(group_half(gpart, j, s, near, i), rb0.at[j, s, i])
                rs(1, j, s, i, group(gpart, j, s, near)).start()
        for s in range(2):
            for i in range(2):
                rs(0, j, s, i, group_half(gpart, j, s, ring(me(1 - s), 2), i)).wait_send()

    def rs2(j):
        for s in range(2):
            m = me(1 - s)
            mine = group(gpart, j, s, m)
            for i in range(2):
                rs(1, j, s, i, mine).wait_recv()
            add(mine, rb1.at[j, s, 0], rb1.at[j, s, 1])
            far = ring(me(s), 2)
            for i in range(2):
                rs(2, j, s, i, block_half(gpart, j, s, far, i)).start()
        for s in range(2):
            for i in range(2):
                rs(1, j, s, i, group(gpart, j, s, ring(me(1 - s), 1 - 2 * i))).wait_send()

    def rs3(j):
        for s in range(2):
            m = me(s)
            for i in range(2):
                rs(2, j, s, i, block_half(gpart, j, s, ring(m, 2), i)).wait_recv()
                near = ring(m, 1 - 2 * i)
                add(block_half(gpart, j, s, near, i), rb2.at[j, s, i])
                rs(3, j, s, i, block(gpart, j, s, near)).start()
        for s in range(2):
            for i in range(2):
                rs(2, j, s, i, block_half(gpart, j, s, ring(me(s), 2), i)).wait_send()

    def rs4(j):
        for s, out in enumerate((gg_ref, ug_ref)):
            mine = block(gpart, j, s, me(s))
            for i in range(2):
                rs(3, j, s, i, mine).wait_recv()
            v = mine[...].astype(F32) + rb3[j, s, 0].astype(F32) + rb3[j, s, 1].astype(F32)
            out[0, :, cols(j)] = v.astype(BF)
        for s in range(2):
            for i in range(2):
                rs(3, j, s, i, block(gpart, j, s, ring(me(s), 1 - 2 * i))).wait_send()

    d_sib = remote(dxs, dxr, d_send.at[0], d_recv.at[0], sib_dev)

    def d_line(s):
        return remote(dxz.at[s - 1], dxq.at[s - 1], d_send.at[s], d_recv.at[s], z_dev(s))

    def dx0():
        for i in range(4):
            dxs[i] = acc[:, feat(2 * i + 1 - k)].astype(BF)
        d_sib.start()

    def dx1():
        d_sib.wait()
        for s in (2, 1, 3):
            zt = ring(zl, s)
            dxz[s - 1] = (acc[:, feat(2 * zt + k)] + dxr[zt].astype(F32)).astype(BF)
            d_line(s).start()

    def dx2():
        v = acc[:, feat(2 * zl + k)] + dxr[zl].astype(F32)
        for s in (1, 2, 3):
            d_line(s).wait()
            v = v + dxq[s - 1].astype(F32)
        dx_ref[...] = v.astype(BF)

    x_start()
    fo = TICKS_TO_FORWARD

    def tick(t, carry):
        def at(off, fn):
            j = t - off

            @pl.when((j >= 0) & (j < nch))
            def _():
                fn(j)

        at(3, ag3)
        at(2, ag2)
        at(1, ag1)
        at(0, ag0)
        pl.when(t == 1)(x_forward)

        @pl.when(t == 3)
        def _():
            x_finish()
            own_cot.wait()

        at(fo + 6, rs4)
        at(fo + 5, rs3)
        at(fo + 4, rs2)
        at(fo + 3, rs1)
        at(fo + 1, deltas)
        at(fo, forward)
        at(fo + 2, grads)
        pl.when(t == nch + fo + 1)(dx0)
        pl.when(t == nch + fo + 2)(dx1)
        pl.when(t == nch + fo + 4)(dx2)
        return carry

    lax.fori_loop(0, nch + fo + 6, tick, 0)


def local(inputs, gate_weight, up_weight, cotangent):
    tok, fb = inputs.shape
    _, rows, width = gate_weight.shape
    half = cotangent.shape[0]
    nch = width // CW
    feats = rows * NX * NX
    vm, dma = pltpu.VMEM, pltpu.SemaphoreType.DMA
    any_spec = pl.BlockSpec(memory_space=pl.ANY)
    vmem_spec = pl.BlockSpec(memory_space=pltpu.VMEM)
    return pl.pallas_call(
        functools.partial(kernel, nch),
        out_shape=(
            jax.ShapeDtypeStruct((half, width), BF),
            jax.ShapeDtypeStruct((tok, fb), BF),
            jax.ShapeDtypeStruct((1, rows, width), BF),
            jax.ShapeDtypeStruct((1, rows, width), BF),
        ),
        in_specs=[any_spec] * 4,
        out_specs=[vmem_spec] * 4,
        scratch_shapes=[
            vm((nch, 2, NX, NX, rows, CW), BF),
            vm((nch, 2, NX, NX, rows, CW), BF),
            vm((nch, 2, 2, 2, rows, CW), BF),
            vm((nch, 2, 2, NX, rows, CW), BF),
            vm((nch, 2, 2, rows // 2, CW), BF),
            vm((nch, 2, 2, rows, CW), BF),
            vm((tok, feats), BF),
            vm((NX, 4 * rows, tok), BF),
            vm((tok, feats), F32),
            vm((nch, 2, half, 2 * CW), BF),
            vm((nch, half, 2 * CW), BF),
            vm((nch, 2, half, 2 * CW), BF),
            vm((half, width), BF),
            vm((4, tok, fb), BF),
            vm((4, tok, fb), BF),
            vm((3, tok, fb), BF),
            vm((3, tok, fb), BF),
            dma((2, nch)),
            dma((2,)),
            dma((4, 2, 2, nch)),
            dma((4, 2, 2, nch)),
            dma((4, 2, 2, nch)),
            dma((4, 2, 2, nch)),
            dma((2, nch)),
            dma((2, nch)),
            dma((7,)),
            dma((7,)),
            dma((4,)),
            dma((4,)),
        ],
        compiler_params=pltpu.CompilerParams(
            collective_id=0, has_side_effects=True, vmem_limit_bytes=62 * 2**20
        ),
    )(inputs, gate_weight, up_weight, cotangent)


def solution(mesh):
    return jax.shard_map(
        local,
        mesh=mesh,
        in_specs=(
            P("depth", ("row", "col")),
            P("row", "depth", "col"),
            P("row", "depth", "col"),
            P(("depth", "row"), "col"),
        ),
        out_specs=(
            P(("depth", "row"), "col"),
            P("depth", ("row", "col")),
            P("row", "depth", "col"),
            P("row", "depth", "col"),
        ),
        check_vma=False,
    )
```

```python
import functools

import jax
import jax.numpy as jnp
from jax import lax
from jax.experimental import pallas as pl
from jax.experimental.pallas import tpu as pltpu
from jax.sharding import PartitionSpec as P

MESH = pl.DeviceIdType.MESH
BF = jnp.bfloat16
F32 = jnp.float32
NX = 4
ROWS = 128
CW = 128
SA = 2
SZ = 2
SR = 2
XF = 2 * SA
WA, WZ, WR = 2 * SA + 2, 2 * SZ + 2, 2 * SR + 2
FIRST = ((0, 2), (2, 6), (6, 14))


def kernel(
    nch, x_hbm, gw_hbm, uw_hbm, cot_hbm, hid_hbm, dx_hbm, gg_hbm, ug_hbm,
    hid_ref, dx_ref, gg_ref, ug_ref, panel, gpart, rb0, rb1, rb2, rb3, xp, xt, acc, part, zin, dl, cot, dxs, dxr, dxz, dxq,
    loc_sem, in_sem, out_sem, first_send, first_recv, ag_send, ag_recv, rs_send, rs_recv, z_send, z_recv, x_send, x_recv, d_send, d_recv,
):
    d, r, c = lax.axis_index("depth"), lax.axis_index("row"), lax.axis_index("col")
    x, y = lax.div(d, NX), lax.rem(d, NX)
    zl, k = lax.div(c, 2), lax.rem(c, 2)
    tok = dx_ref.shape[0]
    half = tok // 2
    fb = dx_ref.shape[1]

    def ring(p, s):
        return lax.rem(p + s + NX, NX)

    def x_dev(s):
        return {"depth": ring(x, s) * NX + y}

    def y_dev(s):
        return {"depth": x * NX + ring(y, s)}

    row_dev = {"row": 1 - r}
    sib_dev = {"col": c + 1 - 2 * k}

    def z_dev(s):
        return {"col": ring(zl, s) * 2 + k}

    def remote(src, dst, ssem, rsem, dev):
        return pltpu.make_async_remote_copy(
            src_ref=src, dst_ref=dst, send_sem=ssem, recv_sem=rsem, device_id=dev, device_id_type=MESH
        )

    def cols(j):
        return pl.ds(pl.multiple_of(j * CW, CW), CW)

    def feat(b):
        return pl.ds(pl.multiple_of(b * fb, fb), fb)

    def send(make, j):
        @pl.when(j >= 2)
        def _():
            make(j - 2).wait_send()

        make(j).start()

    w_hbm = (gw_hbm, uw_hbm)

    def own(j, s):
        return pltpu.make_async_copy(w_hbm[s].at[0, :, cols(j)], panel.at[j, s, x, y], loc_sem.at[s, j])

    own_x = pltpu.make_async_copy(x_hbm, xp.at[:, feat(c)], in_sem.at[0])
    own_cot = pltpu.make_async_copy(cot_hbm, cot, in_sem.at[1])

    def start_own(j, carry):
        for s in range(2):
            own(j, s).start()
        return carry

    own_x.start()
    lax.fori_loop(0, nch, start_own, 0)
    own_cot.start()

    partners = [x_dev(1), x_dev(-1), y_dev(1), y_dev(-1), row_dev, sib_dev, z_dev(1), z_dev(2), z_dev(3)]
    barrier = pltpu.get_barrier_semaphore()
    for dev in partners:
        pl.semaphore_signal(barrier, inc=1, device_id=dev, device_id_type=MESH)
    pl.semaphore_wait(barrier, len(partners))

    def x_line(s, b):
        blk = xp.at[:, feat(b)]
        return remote(blk, blk, x_send.at[s - 1], x_recv.at[s - 1], z_dev(s))

    def x_sib(s, b):
        blk = xp.at[:, feat(b)]
        return remote(blk, blk, x_send.at[3 + s], x_recv.at[3 + s], sib_dev)

    def x_start():
        own_x.wait()
        for s in (1, 2, 3):
            x_line(s, c).start()
        x_sib(0, c).start()

    def x_forward():
        for s in (1, 3, 2):
            b = ring(zl, -s) * 2 + k
            x_line(s, b).wait_recv()
            x_sib(s, b).start()

    def x_finish():
        for s in (1, 2, 3):
            x_line(s, c).wait_send()
        for s in range(4):
            b = ring(zl, -s) * 2 + 1 - k
            x_sib(s, b).wait_recv()
            x_sib(s, c).wait_send()
        for i in range(NX):
            w = 4 * ROWS
            xt[i] = jnp.transpose(xp[:, i * w : (i + 1) * w])

    def ring_dev(axis, s):
        return x_dev(s) if axis == 0 else y_dev(s)

    def me(axis):
        return x if axis == 0 else y

    def block(buf, j, s, p):
        return buf.at[j, 0, p, y] if s == 0 else buf.at[j, 1, x, p]

    def block_half(buf, j, s, p, h):
        rows = pl.ds(h * (ROWS // 2), ROWS // 2)
        return buf.at[j, 0, p, y, rows] if s == 0 else buf.at[j, 1, x, p, rows]

    def group(buf, j, s, q):
        return buf.at[j, 0, :, q] if s == 0 else buf.at[j, 1, q]

    def group_half(buf, j, s, q, h):
        return buf.at[j, 0, pl.ds(2 * h, 2), q] if s == 0 else buf.at[j, 1, q, pl.ds(2 * h, 2)]

    def first_part(n, s, p):
        lo, hi = FIRST[n]
        js = pl.ds(lo, hi - lo)
        return panel.at[js, 0, p, y] if s == 0 else panel.at[js, 1, x, p]

    def first(n, s, i, p):
        src = first_part(n, s, p)
        return remote(src, src, first_send.at[s, i, n], first_recv.at[s, i, n], ring_dev(s, 1 - 2 * i))

    def first_start(n):
        def ready(j, carry):
            for s in range(2):
                own(j, s).wait()
            return carry

        lax.fori_loop(*FIRST[n], ready, 0)
        for s in range(2):
            for i in range(2):
                first(n, s, i, me(s)).start()

    def first_wait(n):
        for s in range(2):
            for i in range(2):
                first(n, s, i, ring(me(s), -1 + 2 * i)).wait_recv()
        for s in range(2):
            for i in range(2):
                first(n, s, i, me(s)).wait_send()

    def ag_ref(stage, j, s, i, shift):
        if stage == 1:
            return block_half(panel, j, s, ring(me(s), shift), i)
        q = ring(me(1 - s), shift)
        return group(panel, j, s, q) if stage == 2 else group_half(panel, j, s, q, i)

    def ag(stage, j, s, i, shift):
        src = ag_ref(stage, j, s, i, shift)
        axis = s if stage == 1 else 1 - s
        return remote(
            src, src, ag_send.at[stage - 1, s, i, lax.rem(j, 2)],
            ag_recv.at[stage - 1, s, i, lax.rem(j, WA)], ring_dev(axis, 1 - 2 * i),
        )

    def ag_out(stage, s, i):
        return lambda j: ag(stage, j, s, i, 0 if stage == 2 else -1 + 2 * i)

    def ag1(j):
        for n in range(len(FIRST)):
            pl.when(j == FIRST[n][0])(functools.partial(first_wait, n))
        for s in range(2):
            for i in range(2):
                send(ag_out(1, s, i), j)

    def ag2(j):
        for s in range(2):
            for i in range(2):
                ag(1, j, s, i, 2).wait_recv()
            for i in range(2):
                send(ag_out(2, s, i), j)

    def ag3(j):
        for s in range(2):
            for i in range(2):
                ag(2, j, s, i, -1 + 2 * i).wait_recv()
                send(ag_out(3, s, i), j)

    def ag4(j):
        for s in range(2):
            for i in range(2):
                ag(3, j, s, i, 2).wait_recv()

    def z1(j):
        return remote(
            part.at[j, 1 - r], zin.at[j], z_send.at[0, lax.rem(j, 2)], z_recv.at[0, lax.rem(j, WZ)], row_dev
        )

    def z2(j, h):
        src = dl.at[j, h]
        return remote(src, src, z_send.at[1, lax.rem(j, 2)], z_recv.at[1, lax.rem(j, WZ)], row_dev)

    def z2_out(j):
        return z2(j, r)

    def weights(j, i):
        n = 4 * ROWS
        return jnp.concatenate([panel[j, 0, i].reshape(n, CW), panel[j, 1, i].reshape(n, CW)], axis=1)

    def forward(j):
        ag4(j)
        w = jnp.concatenate([weights(j, i) for i in range(NX)], axis=0)
        out = jnp.dot(xp[...], w, preferred_element_type=F32)
        part[j] = out.reshape(2, half, 2 * CW).astype(BF)
        send(z1, j)

    def deltas(j):
        z1(j).wait_recv()
        total = part[j, r].astype(F32) + zin[j].astype(F32)
        gate, up = total[:, :CW], total[:, CW:]
        sig = jax.nn.sigmoid(gate)
        act = gate * sig
        hid_ref[:, cols(j)] = (act * up).astype(BF)
        upstream = cot[:, cols(j)].astype(F32)
        gd = (upstream * up * sig * (1.0 + gate * (1.0 - sig))).astype(BF)
        ud = (upstream * act).astype(BF)
        dl[j, r] = jnp.concatenate([gd, ud], axis=1)
        send(z2_out, j)

    def grads(j):
        z2(j, 1 - r).wait_recv()

        def wgrad(i, carry):
            g = jnp.dot(xt[i], dl[j].reshape(tok, 2 * CW), preferred_element_type=F32).astype(BF)
            gpart[j, 0, i] = g[:, :CW].reshape(NX, ROWS, CW)
            gpart[j, 1, i] = g[:, CW:].reshape(NX, ROWS, CW)
            return carry

        lax.fori_loop(0, NX, wgrad, 0)
        rs0(j)

        def dgrad(i, carry):
            w = weights(j, i)
            p = lax.dot_general(
                dl[j].reshape(tok, 2 * CW), w, (((1,), (1,)), ((), ())), preferred_element_type=F32
            )
            sl = pl.ds(pl.multiple_of(i * 4 * ROWS, 4 * ROWS), 4 * ROWS)

            @pl.when(j == 0)
            def _():
                acc[:, sl] = p

            @pl.when(j > 0)
            def _():
                acc[:, sl] += p

            return carry

        lax.fori_loop(0, NX, dgrad, 0)

    def rs_ref(stage, j, s, i):
        m = me(1 - s) if stage < 2 else me(s)
        if stage == 0:
            return group_half(gpart, j, s, ring(m, 2), i)
        if stage == 1:
            return group(gpart, j, s, ring(m, 1 - 2 * i))
        if stage == 2:
            return block_half(gpart, j, s, ring(m, 2), i)
        return block(gpart, j, s, ring(m, 1 - 2 * i))

    def rs(stage, j, s, i):
        axis = 1 - s if stage < 2 else s
        dst = (rb0, rb1, rb2, rb3)[stage].at[j, s, i]
        return remote(
            rs_ref(stage, j, s, i), dst, rs_send.at[stage, s, i, lax.rem(j, 2)],
            rs_recv.at[stage, s, i, lax.rem(j, WR)], ring_dev(axis, 1 - 2 * i),
        )

    def rs_out(stage, s, i):
        return lambda j: rs(stage, j, s, i)

    def add(ref, *others):
        v = ref[...].astype(F32)
        for o in others:
            v = v + o[...].astype(F32)
        ref[...] = v.astype(BF)

    def rs0(j):
        for s in range(2):
            for i in range(2):
                send(rs_out(0, s, i), j)

    def rs1(j):
        for s in range(2):
            for i in range(2):
                rs(0, j, s, i).wait_recv()
                add(group_half(gpart, j, s, ring(me(1 - s), 1 - 2 * i), i), rb0.at[j, s, i])
                send(rs_out(1, s, i), j)

    def rs2(j):
        for s in range(2):
            for i in range(2):
                rs(1, j, s, i).wait_recv()
            add(group(gpart, j, s, me(1 - s)), rb1.at[j, s, 0], rb1.at[j, s, 1])
            for i in range(2):
                send(rs_out(2, s, i), j)

    def rs3(j):
        for s in range(2):
            for i in range(2):
                rs(2, j, s, i).wait_recv()
                add(block_half(gpart, j, s, ring(me(s), 1 - 2 * i), i), rb2.at[j, s, i])
                send(rs_out(3, s, i), j)

    def rs4(j):
        for s, out in enumerate((gg_ref, ug_ref)):
            for i in range(2):
                rs(3, j, s, i).wait_recv()
            v = block(gpart, j, s, me(s))[...].astype(F32)
            v = v + rb3[j, s, 0].astype(F32) + rb3[j, s, 1].astype(F32)
            out[0, :, cols(j)] = v.astype(BF)

    d_sib = remote(dxs, dxr, d_send.at[0], d_recv.at[0], sib_dev)

    def d_line(s):
        return remote(dxz.at[s - 1], dxq.at[s - 1], d_send.at[s], d_recv.at[s], z_dev(s))

    def dx0():
        for i in range(4):
            dxs[i] = acc[:, feat(2 * i + 1 - k)].astype(BF)
        d_sib.start()

    def dx1():
        d_sib.wait()
        for s in (2, 1, 3):
            zt = ring(zl, s)
            dxz[s - 1] = (acc[:, feat(2 * zt + k)] + dxr[zt].astype(F32)).astype(BF)
            d_line(s).start()

    def dx2():
        v = acc[:, feat(2 * zl + k)] + dxr[zl].astype(F32)
        for s in (1, 2, 3):
            d_line(s).wait()
            v = v + dxq[s - 1].astype(F32)
        dx_ref[...] = v.astype(BF)
        result(1).start()

    outs = ((hid_ref, hid_hbm), (dx_ref, dx_hbm), (gg_ref, gg_hbm), (ug_ref, ug_hbm))

    def result(n):
        return pltpu.make_async_copy(*outs[n], out_sem.at[n])

    fo = 3 * SA
    og = fo + 2 * SZ
    last = og + 4 * SR
    x_start()
    first_start(0)
    first_start(1)

    def tick(t, carry):
        def at(off, fn):
            j = t - off

            @pl.when((j >= 0) & (j < nch))
            def _():
                fn(j)

        at(2 * SA, ag3)
        at(SA, ag2)
        at(0, ag1)
        pl.when(t == SA)(functools.partial(first_start, 2))
        pl.when(t == XF)(x_forward)

        @pl.when(t == fo)
        def _():
            x_finish()
            own_cot.wait()

        at(last, rs4)
        at(og + 3 * SR, rs3)
        at(og + 2 * SR, rs2)
        at(og + SR, rs1)
        at(fo + SZ, deltas)
        at(fo, forward)
        at(og, grads)
        pl.when(t == nch - 1 + fo + SZ)(result(0).start)
        pl.when(t == nch - 1 + og)(dx0)
        pl.when(t == nch - 1 + og + SR)(dx1)
        pl.when(t == nch - 1 + og + 2 * SR)(dx2)
        return carry

    lax.fori_loop(0, nch + last, tick, 0)
    result(2).start()
    result(3).start()
    for j in (nch - 2, nch - 1):
        for s in range(2):
            for i in range(2):
                for stage in (1, 2, 3):
                    ag_out(stage, s, i)(j).wait_send()
                for stage in range(4):
                    rs(stage, j, s, i).wait_send()
        z1(j).wait_send()
        z2_out(j).wait_send()
    for n in range(4):
        result(n).wait()


def hand_on(*refs):
    ins, outs, held, in_sem, out_sem = refs[:4], refs[4:8], refs[8:12], refs[12], refs[13]
    reads = [pltpu.make_async_copy(a, b, in_sem.at[n]) for n, (a, b) in enumerate(zip(ins, held))]
    writes = [pltpu.make_async_copy(a, b, out_sem.at[n]) for n, (a, b) in enumerate(zip(held, outs))]
    for read in reads:
        read.start()
    for read, write in zip(reads, writes):
        read.wait()
        write.start()
    for write in writes:
        write.wait()


def local(inputs, gate_weight, up_weight, cotangent):
    tok, fb = inputs.shape
    _, rows, width = gate_weight.shape
    half = cotangent.shape[0]
    nch = width // CW
    feats = rows * NX * NX
    vm, dma = pltpu.VMEM, pltpu.SemaphoreType.DMA
    any_spec = pl.BlockSpec(memory_space=pl.ANY)
    shapes = ((half, width), (tok, fb), (1, rows, width), (1, rows, width))
    out_shape = tuple(jax.ShapeDtypeStruct(shape, BF) for shape in shapes)
    results = pl.pallas_call(
        functools.partial(kernel, nch),
        out_shape=out_shape,
        in_specs=[any_spec] * 4,
        out_specs=[any_spec] * 4,
        scratch_shapes=[
            *(vm(shape, BF) for shape in shapes),
            vm((nch, 2, NX, NX, rows, CW), BF),
            vm((nch, 2, NX, NX, rows, CW), BF),
            vm((nch, 2, 2, 2, rows, CW), BF),
            vm((nch, 2, 2, NX, rows, CW), BF),
            vm((nch, 2, 2, rows // 2, CW), BF),
            vm((nch, 2, 2, rows, CW), BF),
            vm((tok, feats), BF),
            vm((NX, 4 * rows, tok), BF),
            vm((tok, feats), F32),
            vm((nch, 2, half, 2 * CW), BF),
            vm((nch, half, 2 * CW), BF),
            vm((nch, 2, half, 2 * CW), BF),
            vm((half, width), BF),
            vm((4, tok, fb), BF),
            vm((4, tok, fb), BF),
            vm((3, tok, fb), BF),
            vm((3, tok, fb), BF),
            dma((2, nch)),
            dma((2,)),
            dma((4,)),
            dma((2, 2, len(FIRST))),
            dma((2, 2, len(FIRST))),
            dma((3, 2, 2, 2)),
            dma((3, 2, 2, WA)),
            dma((4, 2, 2, 2)),
            dma((4, 2, 2, WR)),
            dma((2, 2)),
            dma((2, WZ)),
            dma((7,)),
            dma((7,)),
            dma((4,)),
            dma((4,)),
        ],
        compiler_params=pltpu.CompilerParams(
            collective_id=0, has_side_effects=True, vmem_limit_bytes=62 * 2**20
        ),
    )(inputs, gate_weight, up_weight, cotangent)
    return pl.pallas_call(
        hand_on,
        out_shape=out_shape,
        in_specs=[any_spec] * 4,
        out_specs=[any_spec] * 4,
        scratch_shapes=[*(vm(shape, BF) for shape in shapes), dma((4,)), dma((4,))],
    )(*results)


def solution(mesh):
    return jax.shard_map(
        local,
        mesh=mesh,
        in_specs=(
            P("depth", ("row", "col")),
            P("row", "depth", "col"),
            P("row", "depth", "col"),
            P(("depth", "row"), "col"),
        ),
        out_specs=(
            P(("depth", "row"), "col"),
            P("depth", ("row", "col")),
            P("row", "depth", "col"),
            P("row", "depth", "col"),
        ),
        check_vma=False,
    )
```

```python
import functools

import jax
import jax.numpy as jnp
from jax import lax
from jax.experimental import pallas as pl
from jax.experimental.pallas import tpu as pltpu
from jax.sharding import PartitionSpec as P

MESH = pl.DeviceIdType.MESH
BF = jnp.bfloat16
F32 = jnp.float32
NX = 4
ROWS = 128
CW = 128
NT = 4
ORDER = (
    (0, 0), (0, 1), (1, 1), (2, 1), (3, 1), (3, 0), (0, 2), (1, 2), (2, 2), (0, 3), (1, 3), (2, 3), (1, 0), (2, 0),
)
UNITS = len(ORDER)
TILES = sum(n << 2 * u for u, (n, _) in enumerate(ORDER))
SHIFTS = sum((0, 2, 1, 3)[m] << 2 * u for u, (_, m) in enumerate(ORDER))
FIRST_OF_TILE = [min(u for u, (n, _) in enumerate(ORDER) if n == i) for i in range(NT)]
LAST_OF_TILE = [max(u for u, (n, _) in enumerate(ORDER) if n == i) for i in range(NT)]
FIRST_OF_GROUP = [min(u for u, (_, m) in enumerate(ORDER) if m == i) for i in range(4)]
LAST_OF_GROUP = [max(u for u, (_, m) in enumerate(ORDER) if m == i) for i in range(4)]
OFF = (2, 1, -1)
SD = 2
SG = 1


def kernel(
    x_hbm, gw_hbm, uw_hbm, cot_hbm, hid_hbm, dx_hbm, gg_hbm, ug_hbm,
    hid, dx, gg, ug, wpk, panel, xp, xt, acc, gacc, gp, rb0, rb1, gr, part, zin, dl, ctb, hb,
    dxs, dxr, dys, dyr, dxz, dxq,
    in_sem, own_sem, out_sem, wa_s, wa_r, wx_s, wx_r, xz_s, xz_r, xy_s, xy_r, xs_s, xs_r, ct_s, ct_r,
    z_s, z_r, rs_s, rs_r, ga_s, ga_r, hd_s, hd_r, ds_s, ds_r, dy_s, dy_r, dz_s, dz_r,
):
    d, r, c = lax.axis_index("depth"), lax.axis_index("row"), lax.axis_index("col")
    x, y = lax.div(d, NX), lax.rem(d, NX)
    zl, k = lax.div(c, 2), lax.rem(c, 2)
    tok, fb = dx.shape
    half = tok // 2

    def ring(p, s):
        return lax.rem(p + s + NX, NX)

    def x_dev(s):
        return {"depth": ring(x, s) * NX + y}

    def y_dev(s):
        return {"depth": x * NX + ring(y, s)}

    row_dev = {"row": 1 - r}
    sib_dev = {"col": c + 1 - 2 * k}

    def z_dev(s):
        return {"col": ring(zl, s) * 2 + k}

    def remote(src, dst, ssem, rsem, dev):
        return pltpu.make_async_remote_copy(
            src_ref=src, dst_ref=dst, send_sem=ssem, recv_sem=rsem, device_id=dev, device_id_type=MESH
        )

    def span(start, n):
        return pl.ds(pl.multiple_of(start * CW, CW), n * CW)

    def first_tile(q):
        return 3 * q + lax.div(q + 1, 2)

    def shared_tile(q):
        return 3 + 7 * lax.div(q, 2)

    def tile_of(q, n):
        return first_tile(q) + n if n < NT - 1 else shared_tile(q)

    def feat(b):
        return pl.ds(pl.multiple_of(b * fb, fb), fb)

    def own(n, s):
        src = (gw_hbm, uw_hbm)[s].at[0, :, span(n, 1)]
        return pltpu.make_async_copy(src, wpk.at[n, :, s * CW : (s + 1) * CW], in_sem.at[1])

    def own_start(n, carry):
        for s in range(2):
            own(n, s).start()
        return carry

    def own_tile(n):
        return pltpu.make_async_copy(wpk.at[tile_of(y, n)], panel.at[n, x, y], own_sem.at[n])

    own_x = pltpu.make_async_copy(x_hbm, xp.at[y, k, :, feat(zl)], in_sem.at[0])
    own_cot = (
        pltpu.make_async_copy(cot_hbm.at[:, span(first_tile(y), 3)], ctb.at[y, :, 0 : 3 * CW], in_sem.at[2]),
        pltpu.make_async_copy(cot_hbm.at[:, span(shared_tile(y), 1)], ctb.at[y, :, 3 * CW :], in_sem.at[3]),
    )
    own_x.start()
    lax.fori_loop(0, wpk.shape[0], own_start, 0)
    for copy in own_cot:
        copy.start()

    partners = [x_dev(1), x_dev(-1), y_dev(1), y_dev(-1), y_dev(2), row_dev, sib_dev, z_dev(1), z_dev(2), z_dev(3)]
    barrier = pltpu.get_barrier_semaphore()
    for dev in partners:
        pl.semaphore_signal(barrier, inc=1, device_id=dev, device_id_type=MESH)
    pl.semaphore_wait(barrier, len(partners))

    def wa(q, n, to, frm):
        return remote(wpk.at[tile_of(to, n)], panel.at[n, x, frm], wa_s.at[q, n], wa_r.at[q, n], y_dev(OFF[q]))

    def wa_start(n):
        own_tile(n).start()
        for q in range(3):
            wa(q, n, ring(y, OFF[q]), y).start()

    def wx(stage, n, i, shift):
        p = ring(x, shift)
        src = panel.at[n, p] if stage == 0 else panel.at[n, p, pl.ds(2 * i, 2)]
        return remote(src, src, wx_s.at[stage, i, n], wx_r.at[stage, i, n], x_dev(1 - 2 * i))

    def wg1(n):
        own_tile(n).wait()
        for q in range(3):
            wa(q, n, y, ring(y, -OFF[q])).wait_recv()
        for i in range(2):
            wx(0, n, i, 0).start()

    def wg2(n):
        for i in range(2):
            wx(0, n, i, -1 + 2 * i).wait_recv()
            wx(1, n, i, -1 + 2 * i).start()

    def wg3(n):
        for i in range(2):
            wx(1, n, i, 2).wait_recv()

    def x_line(s, b):
        blk = xp.at[y, k, :, feat(b)]
        return remote(blk, blk, xz_s.at[s - 1], xz_r.at[s - 1], z_dev(s))

    def x_side(q, n, g):
        blk = xp.at[g, k, :, feat(ring(zl, -n))]
        return remote(blk, blk, xy_s.at[q, n], xy_r.at[q, n], y_dev(OFF[q]))

    def x_sib(n, g, h):
        blk = xp.at[g, h]
        return remote(blk, blk, xs_s.at[n], xs_r.at[n], sib_dev)

    def x_whole(q, g):
        blk = xp.at[g, k]
        return remote(blk, blk, xy_s.at[q, 0], xy_r.at[q, 0], y_dev(OFF[q]))

    def x_arrive(s):
        x_line(s, ring(zl, -s)).wait_recv()
        x_side(0, s, y).start()

    def x_rest():
        for q in (2, 1):
            x_whole(q, y).start()
            ct(q, ring(y, OFF[q]), y).start()

    def x_from(q):
        return ring(y, -OFF[q])

    def x_group(q):
        g = x_from(q)
        if q == 0:
            for n in range(4):
                x_side(q, n, g).wait_recv()
        else:
            x_whole(q, g).wait_recv()
        x_sib(q + 1, g, k).start()

    def x_ready(n, g):
        x_sib(n, g, 1 - k).wait_recv()
        for i in range(NX):
            w = slice(i * fb, (i + 1) * fb)
            xt[g, i] = jnp.concatenate([jnp.transpose(xp[g, 0, :, w]), jnp.transpose(xp[g, 1, :, w])], axis=0)

    def ct(q, to, frm):
        return remote(
            cot_hbm.at[:, span(first_tile(to), 3)], ctb.at[frm, :, 0 : 3 * CW], ct_s.at[q], ct_r.at[q], y_dev(OFF[q])
        )

    def ct_shared(to, frm):
        return remote(
            cot_hbm.at[:, span(shared_tile(to), 1)], ctb.at[frm, :, 3 * CW :], ct_s.at[3], ct_r.at[3], y_dev(2)
        )

    def ct_wait(q):
        if q == 0:
            for copy in own_cot:
                copy.wait()
            ct_shared(y, ring(y, 2)).wait_recv()
        ct(q, y, ring(y, -OFF[q])).wait_recv()

    def unit(u):
        n = lax.rem(lax.shift_right_logical(jnp.int32(TILES), 2 * u), 4)
        shift = lax.rem(lax.shift_right_logical(jnp.int32(SHIFTS), 2 * u), 4)
        return n, lax.rem(y + shift, NX)

    def among(u, units):
        hit = u == units[0]
        for v in units[1:]:
            hit = hit | (u == v)
        return hit

    def z1(u):
        return remote(part.at[u, 1 - r], zin.at[u], z_s.at[0, u], z_r.at[0, u], row_dev)

    def z2(u, h):
        blk = dl.at[u, h]
        return remote(blk, blk, z_s.at[1, u], z_r.at[1, u], row_dev)

    def forward(u):
        n, g = unit(u)
        out = jnp.zeros((tok, 2 * CW), F32)
        for h in range(2):
            w = panel[n, :, 2 * h : 2 * h + 2].reshape(NX * 2 * ROWS, 2 * CW)
            out = out + jnp.dot(xp[g, h], w, preferred_element_type=F32)
        part[u] = out.reshape(2, half, 2 * CW).astype(BF)
        z1(u).start()

    def deltas(u):
        n, g = unit(u)
        z1(u).wait()
        total = part[u, r].astype(F32) + zin[u].astype(F32)
        gate, up = total[:, :CW], total[:, CW:]
        sig = jax.nn.sigmoid(gate)
        act = gate * sig
        hb[g, :, span(n, 1)] = (act * up).astype(BF)
        upstream = ctb[g, :, span(n, 1)].astype(F32)
        gd = (upstream * up * sig * (1.0 + gate * (1.0 - sig))).astype(BF)
        ud = (upstream * act).astype(BF)
        dl[u, r] = jnp.concatenate([gd, ud], axis=1)
        z2(u, r).start()

    def grads(u):
        n, g = unit(u)
        z2(u, 1 - r).wait_recv()
        z2(u, r).wait_send()
        new_tile = among(u, FIRST_OF_TILE)
        new_group = among(u, FIRST_OF_GROUP)

        def wgrad(i, carry):
            v = jnp.dot(xt[g, i], dl[u].reshape(tok, 2 * CW), preferred_element_type=F32)

            @pl.when(new_tile)
            def _():
                gacc[n, i] = v

            @pl.when(jnp.logical_not(new_tile))
            def _():
                gacc[n, i] += v

            return carry

        lax.fori_loop(0, NX, wgrad, 0)

        @pl.when(among(u, LAST_OF_TILE))
        def _():
            def cast(i, carry):
                gp[n, i] = gacc[n, i].reshape(NX, ROWS, 2 * CW).astype(BF)
                return carry

            lax.fori_loop(0, NX, cast, 0)
            for i in range(2):
                rs(0, n, i).start()

        def dgrad(i, carry):
            w = panel[n, i].reshape(NX * ROWS, 2 * CW)
            v = lax.dot_general(
                dl[u].reshape(tok, 2 * CW), w, (((1,), (1,)), ((), ())), preferred_element_type=F32
            )
            sl = pl.ds(pl.multiple_of(i * NX * ROWS, NX * ROWS), NX * ROWS)

            @pl.when(new_group)
            def _():
                acc[g, :, sl] = v

            @pl.when(jnp.logical_not(new_group))
            def _():
                acc[g, :, sl] += v

            return carry

        lax.fori_loop(0, NX, dgrad, 0)

    def rs(stage, n, i):
        src = gp.at[n, ring(x, 2), pl.ds(2 * i, 2)] if stage == 0 else gp.at[n, ring(x, 1 - 2 * i)]
        dst = (rb0, rb1)[stage].at[n, i]
        return remote(src, dst, rs_s.at[stage, i, n], rs_r.at[stage, i, n], x_dev(1 - 2 * i))

    def add(ref, *others):
        v = ref[...].astype(F32)
        for o in others:
            v = v + o[...].astype(F32)
        ref[...] = v.astype(BF)

    def rs1(n):
        for i in range(2):
            rs(0, n, i).wait()
            add(gp.at[n, ring(x, 1 - 2 * i), pl.ds(2 * i, 2)], rb0.at[n, i])
            rs(1, n, i).start()

    def ga(q, n, to, frm):
        return remote(gp.at[n, x, to], gr.at[frm, n], ga_s.at[q, n], ga_r.at[q, n], y_dev(OFF[q]))

    def rs2(n):
        for i in range(2):
            rs(1, n, i).wait()
        add(gp.at[n, x], rb1.at[n, 0], rb1.at[n, 1])
        for q in range(3):
            ga(q, n, ring(y, OFF[q]), y).start()
        gr[y, n] = gp[n, x, y]

    def rs3(n):
        for q in range(3):
            ga(q, n, y, ring(y, -OFF[q])).wait_recv()

        if n < NT - 1:
            for p in range(NX):
                at = slice((3 * p + (p + 1) // 2 + n) * CW, (3 * p + (p + 1) // 2 + n + 1) * CW)
                gg[0, :, at] = gr[p, n, :, :CW]
                ug[0, :, at] = gr[p, n, :, CW:]
        else:
            for p in range(2):
                v = (gr[2 * p, n].astype(F32) + gr[2 * p + 1, n].astype(F32)).astype(BF)
                at = slice((3 + 7 * p) * CW, (4 + 7 * p) * CW)
                gg[0, :, at] = v[:, :CW]
                ug[0, :, at] = v[:, CW:]

    def hd(q, g, frm):
        return remote(
            hb.at[g, :, 0 : 3 * CW], hid.at[:, span(first_tile(frm), 3)], hd_s.at[q], hd_r.at[q], y_dev(OFF[q])
        )

    def hd_shared(g, frm):
        return remote(
            hb.at[g, :, 3 * CW :], hid.at[:, span(shared_tile(frm), 1)], hd_s.at[3], hd_r.at[3], y_dev(2)
        )

    def hidden(q):
        hd(q, ring(y, OFF[q]), y).start()
        if q == 0:
            hd_shared(ring(y, 2), y).start()

    def hidden_own():
        hid[:, span(first_tile(y), 3)] = hb[y, :, 0 : 3 * CW]
        hid[:, span(shared_tile(y), 1)] = hb[y, :, 3 * CW :]

    def hidden_end():
        for q in range(3):
            hd(q, y, ring(y, -OFF[q])).wait_recv()
        hd_shared(y, ring(y, 2)).wait_recv()
        result(0).start()

    def d_sib(m):
        return remote(dxs.at[m], dxr.at[m], ds_s.at[m], ds_r.at[m], sib_dev)

    def d_side(q):
        return remote(dys.at[q], dyr.at[q], dy_s.at[q], dy_r.at[q], y_dev(OFF[q]))

    def d_line(s):
        return remote(dxz.at[s - 1], dxq.at[s - 1], dz_s.at[s - 1], dz_r.at[s - 1], z_dev(s))

    def group_at(m):
        return y if m == 0 else ring(y, OFF[m - 1])

    def dx0(m):
        for i in range(NX):
            dxs[m, i] = acc[group_at(m), :, feat(2 * i + 1 - k)].astype(BF)
        d_sib(m).start()

    def dx1(m):
        d_sib(m).wait()
        for i in range(NX):
            dys[m - 1, i] = (acc[group_at(m), :, feat(2 * i + k)] + dxr[m, i].astype(F32)).astype(BF)
        d_side(m - 1).start()

    def dx_sum(b):
        v = acc[y, :, feat(2 * b + k)] + dxr[0, b].astype(F32)
        for q in range(3):
            v = v + dyr[q, b].astype(F32)
        return v

    def dx2():
        d_sib(0).wait()
        for q in range(3):
            d_side(q).wait()
        for s in (2, 1, 3):
            dxz[s - 1] = dx_sum(ring(zl, s)).astype(BF)
            d_line(s).start()

    def dx3():
        v = dx_sum(zl)
        for s in (1, 2, 3):
            d_line(s).wait()
            v = v + dxq[s - 1].astype(F32)
        dx[...] = v.astype(BF)
        result(1).start()

    outs = ((hid, hid_hbm), (dx, dx_hbm), (gg, gg_hbm), (ug, ug_hbm))

    def result(n):
        return pltpu.make_async_copy(*outs[n], out_sem.at[n])

    own_x.wait()
    for s in (2, 1, 3):
        x_line(s, zl).start()
    pltpu.make_async_copy(wpk, wpk, in_sem.at[1]).wait()
    wa_start(0)
    x_side(0, 0, y).start()
    wa_start(1)
    wg1(0)
    x_arrive(1)
    wa_start(2)
    wg2(0)
    x_arrive(3)
    wg1(1)
    x_arrive(2)
    x_sib(0, y, k).start()
    ct(0, ring(y, 2), y).start()
    ct_shared(ring(y, 2), y).start()
    wa_start(3)
    wg3(0)
    x_ready(0, y)

    og = SD + SG

    def tick(t, carry):
        def on(at, fn, *args):
            pl.when(t == at)(functools.partial(fn, *args))

        def at(off, fn):
            u = t - off

            @pl.when((u >= 0) & (u < UNITS))
            def _():
                fn(u)

        on(SD, ct_wait, 0)
        on(SD + FIRST_OF_GROUP[2], ct_wait, 2)
        on(SD + FIRST_OF_GROUP[3], ct_wait, 1)
        at(SD, deltas)
        on(1, x_ready, 1, ring(y, 2))
        on(2, wg3, 1)
        on(3, wg3, 2)
        on(4, wg3, 3)
        on(FIRST_OF_GROUP[2], x_ready, 3, ring(y, 1))
        on(FIRST_OF_GROUP[3], x_ready, 2, ring(y, -1))
        at(0, forward)
        on(0, wg2, 1)
        on(0, wg1, 2)
        on(0, x_group, 0)
        on(0, x_rest)
        on(1, wg2, 2)
        on(1, wg1, 3)
        on(3, wg2, 3)
        on(FIRST_OF_GROUP[2] - 2, x_group, 2)
        on(FIRST_OF_GROUP[3] - 2, x_group, 1)
        at(og, grads)
        for m in range(4):
            on(og + LAST_OF_GROUP[m], dx0, m)
        on(SD + LAST_OF_GROUP[0], hidden_own)
        for q in range(3):
            on(SD + LAST_OF_GROUP[q + 1], hidden, q)
        for m in range(1, 4):
            on(og + LAST_OF_GROUP[m] + 1, dx1, m)
        on(og + LAST_OF_GROUP[0] + 1, dx2)
        for n, u in enumerate(LAST_OF_TILE):
            on(og + u + 3, rs3, n)
        for n, u in enumerate(LAST_OF_TILE):
            on(og + u + 2, rs2, n)
        for n, u in enumerate(LAST_OF_TILE):
            on(og + u + 1, rs1, n)
        on(og + UNITS + 1, hidden_end)
        on(og + UNITS + 2, dx3)
        return carry

    lax.fori_loop(0, og + UNITS + 3, tick, 0)
    result(2).start()
    result(3).start()
    for n in range(NT):
        for q in range(3):
            wa(q, n, ring(y, OFF[q]), y).wait_send()
            ga(q, n, ring(y, OFF[q]), y).wait_send()
        for i in range(2):
            wx(0, n, i, 0).wait_send()
            wx(1, n, i, -1 + 2 * i).wait_send()
        x_sib(n, y, k).wait_send()
        x_side(0, n, y).wait_send()
    for q in range(3):
        x_line(q + 1, zl).wait_send()
        ct(q, ring(y, OFF[q]), y).wait_send()
        hd(q, ring(y, OFF[q]), y).wait_send()
    ct_shared(ring(y, 2), y).wait_send()
    x_whole(1, y).wait_send()
    x_whole(2, y).wait_send()
    hd_shared(ring(y, 2), y).wait_send()
    for n in range(4):
        result(n).wait()


def hand_on(*refs):
    ins, outs, held, in_sem, out_sem = refs[:4], refs[4:8], refs[8:12], refs[12], refs[13]
    reads = [pltpu.make_async_copy(a, b, in_sem.at[n]) for n, (a, b) in enumerate(zip(ins, held))]
    writes = [pltpu.make_async_copy(a, b, out_sem.at[n]) for n, (a, b) in enumerate(zip(held, outs))]
    for read in reads:
        read.start()
    for read, write in zip(reads, writes):
        read.wait()
        write.start()
    for write in writes:
        write.wait()


def local(inputs, gate_weight, up_weight, cotangent):
    tok, fb = inputs.shape
    _, rows, width = gate_weight.shape
    half = cotangent.shape[0]
    feats = rows * NX * NX
    vm, dma = pltpu.VMEM, pltpu.SemaphoreType.DMA
    any_spec = pl.BlockSpec(memory_space=pl.ANY)
    shapes = ((half, width), (tok, fb), (1, rows, width), (1, rows, width))
    out_shape = tuple(jax.ShapeDtypeStruct(shape, BF) for shape in shapes)
    results = pl.pallas_call(
        kernel,
        out_shape=out_shape,
        in_specs=[any_spec] * 4,
        out_specs=[any_spec] * 4,
        scratch_shapes=[
            *(vm(shape, BF) for shape in shapes),
            vm((width // CW, rows, 2 * CW), BF),
            vm((NT, NX, NX, rows, 2 * CW), BF),
            vm((NX, 2, tok, feats // 2), BF),
            vm((NX, NX, NX * rows, tok), BF),
            vm((NX, tok, feats), F32),
            vm((NT, NX, NX * rows, 2 * CW), F32),
            vm((NT, NX, NX, rows, 2 * CW), BF),
            vm((NT, 2, 2, rows, 2 * CW), BF),
            vm((NT, 2, NX, rows, 2 * CW), BF),
            vm((NX, NT, rows, 2 * CW), BF),
            vm((UNITS, 2, half, 2 * CW), BF),
            vm((UNITS, half, 2 * CW), BF),
            vm((UNITS, 2, half, 2 * CW), BF),
            vm((NX, half, NT * CW), BF),
            vm((NX, half, NT * CW), BF),
            vm((4, 4, tok, fb), BF),
            vm((4, 4, tok, fb), BF),
            vm((3, 4, tok, fb), BF),
            vm((3, 4, tok, fb), BF),
            vm((3, tok, fb), BF),
            vm((3, tok, fb), BF),
            dma((4,)),
            dma((NT,)),
            dma((4,)),
            *(dma((3, NT)) for _ in range(2)),
            *(dma((2, 2, NT)) for _ in range(2)),
            *(dma((3,)) for _ in range(2)),
            *(dma((3, 4)) for _ in range(2)),
            *(dma((4,)) for _ in range(2)),
            *(dma((4,)) for _ in range(2)),
            *(dma((2, UNITS)) for _ in range(2)),
            *(dma((2, 2, NT)) for _ in range(2)),
            *(dma((3, NT)) for _ in range(2)),
            *(dma((4,)) for _ in range(2)),
            *(dma((4,)) for _ in range(2)),
            *(dma((3,)) for _ in range(2)),
            *(dma((3,)) for _ in range(2)),
        ],
        compiler_params=pltpu.CompilerParams(
            collective_id=0, has_side_effects=True, vmem_limit_bytes=62 * 2**20
        ),
    )(inputs, gate_weight, up_weight, cotangent)
    return pl.pallas_call(
        hand_on,
        out_shape=out_shape,
        in_specs=[any_spec] * 4,
        out_specs=[any_spec] * 4,
        scratch_shapes=[*(vm(shape, BF) for shape in shapes), dma((4,)), dma((4,))],
    )(*results)


def solution(mesh):
    return jax.shard_map(
        local,
        mesh=mesh,
        in_specs=(
            P("depth", ("row", "col")),
            P("row", "depth", "col"),
            P("row", "depth", "col"),
            P(("depth", "row"), "col"),
        ),
        out_specs=(
            P(("depth", "row"), "col"),
            P("depth", ("row", "col")),
            P("row", "depth", "col"),
            P("row", "depth", "col"),
        ),
        check_vma=False,
    )
```

```python
import functools

import jax
import jax.numpy as jnp
from jax import lax
from jax.experimental import pallas as pl
from jax.experimental.pallas import tpu as pltpu
from jax.sharding import PartitionSpec as P

MESH = pl.DeviceIdType.MESH
BF = jnp.bfloat16
F32 = jnp.float32
NX = 4
ROWS = 128
CW = 128
NT = 4
ORDER = (
    (0, 0), (0, 1), (1, 1), (2, 1), (3, 1), (3, 0), (0, 2), (1, 2), (2, 2), (0, 3), (1, 3), (2, 3), (1, 0), (2, 0),
)
UNITS = len(ORDER)
TILES = sum(n << 2 * u for u, (n, _) in enumerate(ORDER))
SHIFTS = sum((0, 2, 1, 3)[m] << 2 * u for u, (_, m) in enumerate(ORDER))
FIRST_OF_TILE = [min(u for u, (n, _) in enumerate(ORDER) if n == i) for i in range(NT)]
LAST_OF_TILE = [max(u for u, (n, _) in enumerate(ORDER) if n == i) for i in range(NT)]
FIRST_OF_GROUP = [min(u for u, (_, m) in enumerate(ORDER) if m == i) for i in range(4)]
LAST_OF_GROUP = [max(u for u, (_, m) in enumerate(ORDER) if m == i) for i in range(4)]
OFF = (2, 1, -1)
SD = 2
SG = 1


def kernel(
    x_hbm, gw_hbm, uw_hbm, cot_hbm, hid_hbm, dx_hbm, gg_hbm, ug_hbm,
    hid, dx, gg, ug, wpk, panel, xp, xt, acc, gacc, gp, rb0, rb1, gr, part, zin, dl, ctb, hb,
    dxs, dxr, dys, dyr, dxz, dxq,
    in_sem, own_sem, out_sem, wa_s, wa_r, wx_s, wx_r, xz_s, xz_r, xy_s, xy_r, xs_s, xs_r, ct_s, ct_r,
    z_s, z_r, rs_s, rs_r, ga_s, ga_r, hd_s, hd_r, ds_s, ds_r, dy_s, dy_r, dz_s, dz_r,
):
    d, r, c = lax.axis_index("depth"), lax.axis_index("row"), lax.axis_index("col")
    x, y = lax.div(d, NX), lax.rem(d, NX)
    zl, k = lax.div(c, 2), lax.rem(c, 2)
    tok, fb = dx.shape
    half = tok // 2

    def ring(p, s):
        return lax.rem(p + s + NX, NX)

    def x_dev(s):
        return {"depth": ring(x, s) * NX + y}

    def y_dev(s):
        return {"depth": x * NX + ring(y, s)}

    row_dev = {"row": 1 - r}
    sib_dev = {"col": c + 1 - 2 * k}

    def z_dev(s):
        return {"col": ring(zl, s) * 2 + k}

    def remote(src, dst, ssem, rsem, dev):
        return pltpu.make_async_remote_copy(
            src_ref=src, dst_ref=dst, send_sem=ssem, recv_sem=rsem, device_id=dev, device_id_type=MESH
        )

    def span(start, n):
        return pl.ds(pl.multiple_of(start * CW, CW), n * CW)

    def first_tile(q):
        return 3 * q + lax.div(q + 1, 2)

    def shared_tile(q):
        return 3 + 7 * lax.div(q, 2)

    def tile_of(q, n):
        return first_tile(q) + n if n < NT - 1 else shared_tile(q)

    def feat(b):
        return pl.ds(pl.multiple_of(b * fb, fb), fb)

    def own(n, s):
        src = (gw_hbm, uw_hbm)[s].at[0, :, span(n, 1)]
        return pltpu.make_async_copy(src, wpk.at[n, :, s * CW : (s + 1) * CW], in_sem.at[1])

    def own_start(n, carry):
        for s in range(2):
            own(n, s).start()
        return carry

    def own_tile(n):
        return pltpu.make_async_copy(wpk.at[tile_of(y, n)], panel.at[n, x, y], own_sem.at[n])

    own_x = pltpu.make_async_copy(x_hbm, xp.at[y, k, :, feat(zl)], in_sem.at[0])
    own_cot = (
        pltpu.make_async_copy(cot_hbm.at[:, span(first_tile(y), 3)], ctb.at[y, :, 0 : 3 * CW], in_sem.at[2]),
        pltpu.make_async_copy(cot_hbm.at[:, span(shared_tile(y), 1)], ctb.at[y, :, 3 * CW :], in_sem.at[3]),
    )
    own_x.start()
    lax.fori_loop(0, wpk.shape[0], own_start, 0)
    for copy in own_cot:
        copy.start()

    partners = [x_dev(1), x_dev(-1), y_dev(1), y_dev(-1), y_dev(2), row_dev, sib_dev, z_dev(1), z_dev(2), z_dev(3)]
    barrier = pltpu.get_barrier_semaphore()
    for dev in partners:
        pl.semaphore_signal(barrier, inc=1, device_id=dev, device_id_type=MESH)
    pl.semaphore_wait(barrier, len(partners))

    def wa(q, n, to, frm):
        return remote(wpk.at[tile_of(to, n)], panel.at[n, x, frm], wa_s.at[q, n], wa_r.at[q, n], y_dev(OFF[q]))

    def wa_start(n):
        own_tile(n).start()
        for q in range(3):
            wa(q, n, ring(y, OFF[q]), y).start()

    def wx(stage, n, i, shift):
        p = ring(x, shift)
        src = panel.at[n, p] if stage == 0 else panel.at[n, p, pl.ds(2 * i, 2)]
        return remote(src, src, wx_s.at[stage, i, n], wx_r.at[stage, i, n], x_dev(1 - 2 * i))

    def wg1(n):
        own_tile(n).wait()
        for q in range(3):
            wa(q, n, y, ring(y, -OFF[q])).wait_recv()
        for i in range(2):
            wx(0, n, i, 0).start()

    def wg2(n):
        for i in range(2):
            wx(0, n, i, -1 + 2 * i).wait_recv()
            wx(1, n, i, -1 + 2 * i).start()

    def wg3(n):
        for i in range(2):
            wx(1, n, i, 2).wait_recv()

    def x_line(s, b):
        blk = xp.at[y, k, :, feat(b)]
        return remote(blk, blk, xz_s.at[s - 1], xz_r.at[s - 1], z_dev(s))

    def x_side(q, n, g):
        blk = xp.at[g, k, :, feat(ring(zl, -n))]
        return remote(blk, blk, xy_s.at[q, n], xy_r.at[q, n], y_dev(OFF[q]))

    def x_sib(n, g, h):
        blk = xp.at[g, h]
        return remote(blk, blk, xs_s.at[n], xs_r.at[n], sib_dev)

    def x_whole(q, g):
        blk = xp.at[g, k]
        return remote(blk, blk, xy_s.at[q, 0], xy_r.at[q, 0], y_dev(OFF[q]))

    def x_arrive(s):
        x_line(s, ring(zl, -s)).wait_recv()
        x_side(0, s, y).start()

    def x_rest():
        for q in (2, 1):
            x_whole(q, y).start()
            ct(q, ring(y, OFF[q]), y).start()

    def x_from(q):
        return ring(y, -OFF[q])

    def x_group(q):
        g = x_from(q)
        if q == 0:
            for n in range(4):
                x_side(q, n, g).wait_recv()
        else:
            x_whole(q, g).wait_recv()
        x_sib(q + 1, g, k).start()

    def x_ready(n, g):
        x_sib(n, g, 1 - k).wait_recv()
        for i in range(NX):
            w = slice(i * fb, (i + 1) * fb)
            xt[g, i] = jnp.concatenate([jnp.transpose(xp[g, 0, :, w]), jnp.transpose(xp[g, 1, :, w])], axis=0)

    def ct(q, to, frm):
        return remote(
            cot_hbm.at[:, span(first_tile(to), 3)], ctb.at[frm, :, 0 : 3 * CW], ct_s.at[q], ct_r.at[q], y_dev(OFF[q])
        )

    def ct_shared(to, frm):
        return remote(
            cot_hbm.at[:, span(shared_tile(to), 1)], ctb.at[frm, :, 3 * CW :], ct_s.at[3], ct_r.at[3], y_dev(2)
        )

    def ct_wait(q):
        if q == 0:
            ct_shared(y, ring(y, 2)).wait_recv()
        ct(q, y, ring(y, -OFF[q])).wait_recv()

    def unit(u):
        n = lax.rem(lax.shift_right_logical(jnp.int32(TILES), 2 * u), 4)
        shift = lax.rem(lax.shift_right_logical(jnp.int32(SHIFTS), 2 * u), 4)
        return n, lax.rem(y + shift, NX)

    def among(u, units):
        hit = u == units[0]
        for v in units[1:]:
            hit = hit | (u == v)
        return hit

    def z1(u):
        return remote(part.at[u, 1 - r], zin.at[u], z_s.at[0, u], z_r.at[0, u], row_dev)

    def z2(u, h):
        blk = dl.at[u, h]
        return remote(blk, blk, z_s.at[1, u], z_r.at[1, u], row_dev)

    def forward(u):
        n, g = unit(u)
        out = jnp.zeros((tok, 2 * CW), F32)
        for h in range(2):
            w = panel[n, :, 2 * h : 2 * h + 2].reshape(NX * 2 * ROWS, 2 * CW)
            out = out + jnp.dot(xp[g, h], w, preferred_element_type=F32)
        part[u] = out.reshape(2, half, 2 * CW).astype(BF)
        z1(u).start()

    def deltas(u):
        n, g = unit(u)
        z1(u).wait()
        total = part[u, r].astype(F32) + zin[u].astype(F32)
        gate, up = total[:, :CW], total[:, CW:]
        sig = jax.nn.sigmoid(gate)
        act = gate * sig
        hb[g, :, span(n, 1)] = (act * up).astype(BF)
        upstream = ctb[g, :, span(n, 1)].astype(F32)
        gd = (upstream * up * sig * (1.0 + gate * (1.0 - sig))).astype(BF)
        ud = (upstream * act).astype(BF)
        dl[u, r] = jnp.concatenate([gd, ud], axis=1)
        z2(u, r).start()

    def grads(u):
        n, g = unit(u)
        z2(u, 1 - r).wait_recv()
        z2(u, r).wait_send()
        new_tile = among(u, FIRST_OF_TILE)
        new_group = among(u, FIRST_OF_GROUP)
        last = among(u, LAST_OF_TILE)

        def wgrad(i, carry):
            p = ring(x, 2 + i)
            v = jnp.dot(xt[g, p], dl[u].reshape(tok, 2 * CW), preferred_element_type=F32)

            @pl.when(new_tile)
            def _():
                gacc[n, p] = v

            @pl.when(jnp.logical_not(new_tile))
            def _():
                gacc[n, p] += v

            @pl.when(last)
            def _():
                gp[n, p] = gacc[n, p].reshape(NX, ROWS, 2 * CW).astype(BF)

            @pl.when(last & (i == 0))
            def _():
                for h in range(2):
                    rs(0, n, h).start()

            return carry

        lax.fori_loop(0, NX, wgrad, 0)

        def dgrad(i, carry):
            w = panel[n, i].reshape(NX * ROWS, 2 * CW)
            v = lax.dot_general(
                dl[u].reshape(tok, 2 * CW), w, (((1,), (1,)), ((), ())), preferred_element_type=F32
            )
            sl = pl.ds(pl.multiple_of(i * NX * ROWS, NX * ROWS), NX * ROWS)

            @pl.when(new_group)
            def _():
                acc[g, :, sl] = v

            @pl.when(jnp.logical_not(new_group))
            def _():
                acc[g, :, sl] += v

            return carry

        lax.fori_loop(0, NX, dgrad, 0)

    def rs(stage, n, i):
        src = gp.at[n, ring(x, 2), pl.ds(2 * i, 2)] if stage == 0 else gp.at[n, ring(x, 1 - 2 * i)]
        dst = (rb0, rb1)[stage].at[n, i]
        return remote(src, dst, rs_s.at[stage, i, n], rs_r.at[stage, i, n], x_dev(1 - 2 * i))

    def add(ref, *others):
        v = ref[...].astype(F32)
        for o in others:
            v = v + o[...].astype(F32)
        ref[...] = v.astype(BF)

    def rs1(n):
        for i in range(2):
            rs(0, n, i).wait()
            add(gp.at[n, ring(x, 1 - 2 * i), pl.ds(2 * i, 2)], rb0.at[n, i])
            rs(1, n, i).start()

    def ga(q, n, to, frm):
        return remote(gp.at[n, x, to], gr.at[frm, n], ga_s.at[q, n], ga_r.at[q, n], y_dev(OFF[q]))

    def rs2(n):
        for i in range(2):
            rs(1, n, i).wait()
        add(gp.at[n, x], rb1.at[n, 0], rb1.at[n, 1])
        for q in range(3):
            ga(q, n, ring(y, OFF[q]), y).start()
        gr[y, n] = gp[n, x, y]

    def rs3(n):
        for q in range(3):
            ga(q, n, y, ring(y, -OFF[q])).wait_recv()

        if n < NT - 1:
            for p in range(NX):
                at = slice((3 * p + (p + 1) // 2 + n) * CW, (3 * p + (p + 1) // 2 + n + 1) * CW)
                gg[0, :, at] = gr[p, n, :, :CW]
                ug[0, :, at] = gr[p, n, :, CW:]
        else:
            for p in range(2):
                v = (gr[2 * p, n].astype(F32) + gr[2 * p + 1, n].astype(F32)).astype(BF)
                at = slice((3 + 7 * p) * CW, (4 + 7 * p) * CW)
                gg[0, :, at] = v[:, :CW]
                ug[0, :, at] = v[:, CW:]

    def hd(q, g, frm):
        return remote(
            hb.at[g, :, 0 : 3 * CW], hid.at[:, span(first_tile(frm), 3)], hd_s.at[q], hd_r.at[q], y_dev(OFF[q])
        )

    def hd_shared(g, frm):
        return remote(
            hb.at[g, :, 3 * CW :], hid.at[:, span(shared_tile(frm), 1)], hd_s.at[3], hd_r.at[3], y_dev(2)
        )

    def hidden(q):
        hd(q, ring(y, OFF[q]), y).start()
        if q == 0:
            hd_shared(ring(y, 2), y).start()

    def hidden_own():
        hid[:, span(first_tile(y), 3)] = hb[y, :, 0 : 3 * CW]
        hid[:, span(shared_tile(y), 1)] = hb[y, :, 3 * CW :]

    def hidden_end():
        for q in range(3):
            hd(q, y, ring(y, -OFF[q])).wait_recv()
        hd_shared(y, ring(y, 2)).wait_recv()
        result(0).start()

    def d_sib(m):
        return remote(dxs.at[m], dxr.at[m], ds_s.at[m], ds_r.at[m], sib_dev)

    def d_side(q, s):
        b = ring(zl, s)
        return remote(dys.at[q, b], dyr.at[q, b], dy_s.at[q, s], dy_r.at[q, s], y_dev(OFF[q]))

    def d_line(s):
        return remote(dxz.at[s - 1], dxq.at[s - 1], dz_s.at[s - 1], dz_r.at[s - 1], z_dev(s))

    def group_at(m):
        return y if m == 0 else ring(y, OFF[m - 1])

    def dx0(m):
        for i in range(NX):
            dxs[m, i] = acc[group_at(m), :, feat(2 * i + 1 - k)].astype(BF)
        d_sib(m).start()

    def dx1(m):
        d_sib(m).wait()
        for s in (2, 1, 3, 0):
            b = ring(zl, s)
            dys[m - 1, b] = (acc[group_at(m), :, feat(2 * b + k)] + dxr[m, b].astype(F32)).astype(BF)
            d_side(m - 1, s).start()

    def dx_sum(b):
        v = acc[y, :, feat(2 * b + k)] + dxr[0, b].astype(F32)
        for q in range(3):
            v = v + dyr[q, b].astype(F32)
        return v

    def dx2():
        d_sib(0).wait()
        for s in (2, 1, 3):
            for q in range(3):
                d_side(q, s).wait()
            dxz[s - 1] = dx_sum(ring(zl, s)).astype(BF)
            d_line(s).start()

    def dx3():
        for q in range(3):
            d_side(q, 0).wait()
        v = dx_sum(zl)
        for s in (1, 2, 3):
            d_line(s).wait()
            v = v + dxq[s - 1].astype(F32)
        dx[...] = v.astype(BF)
        result(1).start()

    outs = ((hid, hid_hbm), (dx, dx_hbm), (gg, gg_hbm), (ug, ug_hbm))

    def result(n):
        return pltpu.make_async_copy(*outs[n], out_sem.at[n])

    own_x.wait()
    for s in (2, 1, 3):
        x_line(s, zl).start()
    pltpu.make_async_copy(wpk, wpk, in_sem.at[1]).wait()
    wa_start(0)
    wa_start(1)
    x_side(0, 0, y).start()
    wa_start(2)
    wa_start(3)
    wg1(0)
    x_arrive(1)
    wg2(0)
    wg1(1)
    x_arrive(3)
    x_arrive(2)
    x_sib(0, y, k).start()
    ct(0, ring(y, 2), y).start()
    ct_shared(ring(y, 2), y).start()
    for copy in own_cot:
        copy.wait()
    wg3(0)
    x_ready(0, y)

    def settle():
        for n in range(NT):
            for q in range(3):
                wa(q, n, ring(y, OFF[q]), y).wait_send()
            for i in range(2):
                wx(0, n, i, 0).wait_send()
                wx(1, n, i, -1 + 2 * i).wait_send()
            x_sib(n, y, k).wait_send()
            x_side(0, n, y).wait_send()
        for q in range(3):
            x_line(q + 1, zl).wait_send()
            ct(q, ring(y, OFF[q]), y).wait_send()
        ct_shared(ring(y, 2), y).wait_send()
        x_whole(1, y).wait_send()
        x_whole(2, y).wait_send()

    og = SD + SG

    def tick(t, carry):
        def on(at, fn, *args):
            pl.when(t == at)(functools.partial(fn, *args))

        def at(off, fn):
            u = t - off

            @pl.when((u >= 0) & (u < UNITS))
            def _():
                fn(u)

        on(SD + FIRST_OF_GROUP[2], ct_wait, 2)
        on(SD + FIRST_OF_GROUP[3], ct_wait, 1)
        on(1, deltas, 0)
        on(SD + FIRST_OF_GROUP[1], ct_wait, 0)
        pl.when((t > SD) & (t < UNITS + SD - 1))(lambda: deltas(t - SD))
        on(1, x_ready, 1, ring(y, 2))
        on(2, wg3, 1)
        on(3, wg3, 2)
        on(4, wg3, 3)
        on(FIRST_OF_GROUP[2], x_ready, 3, ring(y, 1))
        on(FIRST_OF_GROUP[3], x_ready, 2, ring(y, -1))
        at(0, forward)
        on(0, wg2, 1)
        on(0, wg1, 2)
        on(0, x_group, 0)
        on(0, x_rest)
        on(1, wg2, 2)
        on(1, wg1, 3)
        on(3, wg2, 3)
        on(FIRST_OF_GROUP[2] - 2, x_group, 2)
        on(FIRST_OF_GROUP[3] - 2, x_group, 1)
        for n, u in enumerate(LAST_OF_TILE):
            if u < UNITS - 1:
                on(og + u + 1, rs1, n)
        at(og, grads)
        on(UNITS + SD - 2, deltas, UNITS - 1)
        for m in range(4):
            on(og + LAST_OF_GROUP[m], dx0, m)
        on(SD + LAST_OF_GROUP[0], hidden_own)
        for q in range(3):
            on(SD + LAST_OF_GROUP[q + 1], hidden, q)
        for m in range(1, 4):
            on(og + LAST_OF_GROUP[m] + 1, dx1, m)
        on(og + UNITS, rs1, ORDER[-1][0])
        on(og + LAST_OF_GROUP[0] + 1, dx2)
        for n, u in enumerate(LAST_OF_TILE):
            on(og + u + 3, rs3, n)
        for n, u in enumerate(LAST_OF_TILE):
            on(og + u + 2, rs2, n)
        on(UNITS - 1, settle)
        on(og + UNITS + 1, hidden_end)
        on(og + UNITS + 2, dx3)
        return carry

    lax.fori_loop(0, og + UNITS + 3, tick, 0)
    result(2).start()
    result(3).start()
    for q in range(3):
        for n in range(NT):
            ga(q, n, ring(y, OFF[q]), y).wait_send()
        hd(q, ring(y, OFF[q]), y).wait_send()
    hd_shared(ring(y, 2), y).wait_send()
    for n in range(4):
        result(n).wait()


def hand_on(*refs):
    ins, outs, held, in_sem, out_sem = refs[:4], refs[4:8], refs[8:12], refs[12], refs[13]
    reads = [pltpu.make_async_copy(a, b, in_sem.at[n]) for n, (a, b) in enumerate(zip(ins, held))]
    writes = [pltpu.make_async_copy(a, b, out_sem.at[n]) for n, (a, b) in enumerate(zip(held, outs))]
    for read in reads:
        read.start()
    for read, write in zip(reads, writes):
        read.wait()
        write.start()
    for write in writes:
        write.wait()


def local(inputs, gate_weight, up_weight, cotangent):
    tok, fb = inputs.shape
    _, rows, width = gate_weight.shape
    half = cotangent.shape[0]
    feats = rows * NX * NX
    vm, dma = pltpu.VMEM, pltpu.SemaphoreType.DMA
    any_spec = pl.BlockSpec(memory_space=pl.ANY)
    shapes = ((half, width), (tok, fb), (1, rows, width), (1, rows, width))
    out_shape = tuple(jax.ShapeDtypeStruct(shape, BF) for shape in shapes)
    results = pl.pallas_call(
        kernel,
        out_shape=out_shape,
        in_specs=[any_spec] * 4,
        out_specs=[any_spec] * 4,
        scratch_shapes=[
            *(vm(shape, BF) for shape in shapes),
            vm((width // CW, rows, 2 * CW), BF),
            vm((NT, NX, NX, rows, 2 * CW), BF),
            vm((NX, 2, tok, feats // 2), BF),
            vm((NX, NX, NX * rows, tok), BF),
            vm((NX, tok, feats), F32),
            vm((NT, NX, NX * rows, 2 * CW), F32),
            vm((NT, NX, NX, rows, 2 * CW), BF),
            vm((NT, 2, 2, rows, 2 * CW), BF),
            vm((NT, 2, NX, rows, 2 * CW), BF),
            vm((NX, NT, rows, 2 * CW), BF),
            vm((UNITS, 2, half, 2 * CW), BF),
            vm((UNITS, half, 2 * CW), BF),
            vm((UNITS, 2, half, 2 * CW), BF),
            vm((NX, half, NT * CW), BF),
            vm((NX, half, NT * CW), BF),
            vm((4, 4, tok, fb), BF),
            vm((4, 4, tok, fb), BF),
            vm((3, 4, tok, fb), BF),
            vm((3, 4, tok, fb), BF),
            vm((3, tok, fb), BF),
            vm((3, tok, fb), BF),
            dma((4,)),
            dma((NT,)),
            dma((4,)),
            *(dma((3, NT)) for _ in range(2)),
            *(dma((2, 2, NT)) for _ in range(2)),
            *(dma((3,)) for _ in range(2)),
            *(dma((3, 4)) for _ in range(2)),
            *(dma((4,)) for _ in range(2)),
            *(dma((4,)) for _ in range(2)),
            *(dma((2, UNITS)) for _ in range(2)),
            *(dma((2, 2, NT)) for _ in range(2)),
            *(dma((3, NT)) for _ in range(2)),
            *(dma((4,)) for _ in range(2)),
            *(dma((4,)) for _ in range(2)),
            *(dma((3, 4)) for _ in range(2)),
            *(dma((3,)) for _ in range(2)),
        ],
        compiler_params=pltpu.CompilerParams(
            collective_id=0, has_side_effects=True, vmem_limit_bytes=62 * 2**20
        ),
    )(inputs, gate_weight, up_weight, cotangent)
    return pl.pallas_call(
        hand_on,
        out_shape=out_shape,
        in_specs=[any_spec] * 4,
        out_specs=[any_spec] * 4,
        scratch_shapes=[*(vm(shape, BF) for shape in shapes), dma((4,)), dma((4,))],
    )(*results)


def solution(mesh):
    return jax.shard_map(
        local,
        mesh=mesh,
        in_specs=(
            P("depth", ("row", "col")),
            P("row", "depth", "col"),
            P("row", "depth", "col"),
            P(("depth", "row"), "col"),
        ),
        out_specs=(
            P(("depth", "row"), "col"),
            P("depth", ("row", "col")),
            P("row", "depth", "col"),
            P("row", "depth", "col"),
        ),
        check_vma=False,
    )
```

```python
import functools

import jax
import jax.numpy as jnp
from jax import lax
from jax.experimental import pallas as pl
from jax.experimental.pallas import tpu as pltpu
from jax.sharding import PartitionSpec as P

MESH = pl.DeviceIdType.MESH
BF = jnp.bfloat16
F32 = jnp.float32
NX = 4
ROWS = 128
CW = 128
NT = 4
ORDER = (
    (0, 0), (0, 1), (1, 1), (2, 1), (3, 1), (3, 0), (0, 2), (0, 3), (1, 2), (1, 3),
    (2, 2), (2, 3), (1, 0), (2, 0),
)
UNITS = len(ORDER)
TILES = sum(n << 2 * u for u, (n, _) in enumerate(ORDER))
SHIFTS = sum((0, 2, 1, 3)[m] << 2 * u for u, (_, m) in enumerate(ORDER))
FIRST_OF_TILE = [min(u for u, (n, _) in enumerate(ORDER) if n == i) for i in range(NT)]
LAST_OF_TILE = [max(u for u, (n, _) in enumerate(ORDER) if n == i) for i in range(NT)]
FIRST_OF_GROUP = [min(u for u, (_, m) in enumerate(ORDER) if m == i) for i in range(4)]
LAST_OF_GROUP = [max(u for u, (_, m) in enumerate(ORDER) if m == i) for i in range(4)]
OFF = (2, 1, -1)
SD = 2
SG = 1


def kernel(
    x_hbm, gw_hbm, uw_hbm, cot_hbm, hid_hbm, dx_hbm, gg_hbm, ug_hbm,
    hid, dx, gg, ug, wpk, panel, xp, xt, acc, gacc, gp, rb0, rb1, gr, part, zin, dl, ctb, hb,
    dxs, dxr, dys, dyr, dxz, dxq,
    in_sem, own_sem, out_sem, wa_s, wa_r, wx_s, wx_r, xz_s, xz_r, xy_s, xy_r, xs_s, xs_r, ct_s, ct_r,
    z_s, z_r, rs_s, rs_r, ga_s, ga_r, hd_s, hd_r, ds_s, ds_r, do_s, do_r, dy_s, dy_r, dz_s, dz_r,
):
    d, r, c = lax.axis_index("depth"), lax.axis_index("row"), lax.axis_index("col")
    x, y = lax.div(d, NX), lax.rem(d, NX)
    zl, k = lax.div(c, 2), lax.rem(c, 2)
    tok, fb = dx.shape
    half = tok // 2

    def ring(p, s):
        return lax.rem(p + s + NX, NX)

    def x_dev(s):
        return {"depth": ring(x, s) * NX + y}

    def y_dev(s):
        return {"depth": x * NX + ring(y, s)}

    row_dev = {"row": 1 - r}
    sib_dev = {"col": c + 1 - 2 * k}

    def z_dev(s):
        return {"col": ring(zl, s) * 2 + k}

    def remote(src, dst, ssem, rsem, dev):
        return pltpu.make_async_remote_copy(
            src_ref=src, dst_ref=dst, send_sem=ssem, recv_sem=rsem, device_id=dev, device_id_type=MESH
        )

    def span(start, n):
        return pl.ds(pl.multiple_of(start * CW, CW), n * CW)

    def first_tile(q):
        return 3 * q + lax.div(q + 1, 2)

    def shared_tile(q):
        return 3 + 7 * lax.div(q, 2)

    def tile_of(q, n):
        return first_tile(q) + n if n < NT - 1 else shared_tile(q)

    def feat(b):
        return pl.ds(pl.multiple_of(b * fb, fb), fb)

    def own(n, s):
        src = (gw_hbm, uw_hbm)[s].at[0, :, span(n, 1)]
        return pltpu.make_async_copy(src, wpk.at[n, :, s * CW : (s + 1) * CW], in_sem.at[1])

    def own_start(n, carry):
        for s in range(2):
            own(n, s).start()
        return carry

    def own_tile(n):
        return pltpu.make_async_copy(wpk.at[tile_of(y, n)], panel.at[n, x, y], own_sem.at[n])

    own_x = pltpu.make_async_copy(x_hbm, xp.at[y, k, :, feat(zl)], in_sem.at[0])
    own_cot = (
        pltpu.make_async_copy(cot_hbm.at[:, span(first_tile(y), 3)], ctb.at[y, :, 0 : 3 * CW], in_sem.at[2]),
        pltpu.make_async_copy(cot_hbm.at[:, span(shared_tile(y), 1)], ctb.at[y, :, 3 * CW :], in_sem.at[3]),
    )
    own_x.start()
    lax.fori_loop(0, wpk.shape[0], own_start, 0)
    for copy in own_cot:
        copy.start()

    partners = [x_dev(1), x_dev(-1), y_dev(1), y_dev(-1), y_dev(2), row_dev, sib_dev, z_dev(1), z_dev(2), z_dev(3)]
    barrier = pltpu.get_barrier_semaphore()
    for dev in partners:
        pl.semaphore_signal(barrier, inc=1, device_id=dev, device_id_type=MESH)
    pl.semaphore_wait(barrier, len(partners))

    def wa(q, n, to, frm):
        return remote(wpk.at[tile_of(to, n)], panel.at[n, x, frm], wa_s.at[q, n], wa_r.at[q, n], y_dev(OFF[q]))

    def wa_start(n):
        own_tile(n).start()
        for q in range(3):
            wa(q, n, ring(y, OFF[q]), y).start()

    def wx(stage, n, i, shift):
        p = ring(x, shift)
        src = panel.at[n, p] if stage == 0 else panel.at[n, p, pl.ds(2 * i, 2)]
        return remote(src, src, wx_s.at[stage, i, n], wx_r.at[stage, i, n], x_dev(1 - 2 * i))

    def wg1(n):
        own_tile(n).wait()
        for q in range(3):
            wa(q, n, y, ring(y, -OFF[q])).wait_recv()
        for i in range(2):
            wx(0, n, i, 0).start()

    def wg2(n):
        for i in range(2):
            wx(0, n, i, -1 + 2 * i).wait_recv()
            wx(1, n, i, -1 + 2 * i).start()

    def wg3(n):
        for i in range(2):
            wx(1, n, i, 2).wait_recv()

    def x_line(s, b):
        blk = xp.at[y, k, :, feat(b)]
        return remote(blk, blk, xz_s.at[s - 1], xz_r.at[s - 1], z_dev(s))

    def x_side(q, n, g):
        blk = xp.at[g, k, :, feat(ring(zl, -n))]
        return remote(blk, blk, xy_s.at[q, n], xy_r.at[q, n], y_dev(OFF[q]))

    def x_sib(n, g, h):
        blk = xp.at[g, h]
        return remote(blk, blk, xs_s.at[n], xs_r.at[n], sib_dev)

    def x_whole(q, g):
        blk = xp.at[g, k]
        return remote(blk, blk, xy_s.at[q, 0], xy_r.at[q, 0], y_dev(OFF[q]))

    def x_arrive(s):
        x_line(s, ring(zl, -s)).wait_recv()
        x_side(0, s, y).start()

    def x_rest():
        for q in (2, 1):
            x_whole(q, y).start()
            ct(q, ring(y, OFF[q]), y).start()

    def x_from(q):
        return ring(y, -OFF[q])

    def x_group(q):
        g = x_from(q)
        if q == 0:
            for n in range(4):
                x_side(q, n, g).wait_recv()
        else:
            x_whole(q, g).wait_recv()
        x_sib(q + 1, g, k).start()

    def x_ready(n, g):
        x_sib(n, g, 1 - k).wait_recv()
        for i in range(NX):
            w = slice(i * fb, (i + 1) * fb)
            xt[g, i] = jnp.concatenate([jnp.transpose(xp[g, 0, :, w]), jnp.transpose(xp[g, 1, :, w])], axis=0)

    def ct(q, to, frm):
        return remote(
            cot_hbm.at[:, span(first_tile(to), 3)], ctb.at[frm, :, 0 : 3 * CW], ct_s.at[q], ct_r.at[q], y_dev(OFF[q])
        )

    def ct_shared(to, frm):
        return remote(
            cot_hbm.at[:, span(shared_tile(to), 1)], ctb.at[frm, :, 3 * CW :], ct_s.at[3], ct_r.at[3], y_dev(2)
        )

    def ct_wait(q):
        if q == 0:
            ct_shared(y, ring(y, 2)).wait_recv()
        ct(q, y, ring(y, -OFF[q])).wait_recv()

    def unit(u):
        n = lax.rem(lax.shift_right_logical(jnp.int32(TILES), 2 * u), 4)
        shift = lax.rem(lax.shift_right_logical(jnp.int32(SHIFTS), 2 * u), 4)
        return n, lax.rem(y + shift, NX)

    def among(u, units):
        hit = u == units[0]
        for v in units[1:]:
            hit = hit | (u == v)
        return hit

    def z1(u):
        return remote(part.at[u, 1 - r], zin.at[u], z_s.at[0, u], z_r.at[0, u], row_dev)

    def z2(u, h):
        blk = dl.at[u, h]
        return remote(blk, blk, z_s.at[1, u], z_r.at[1, u], row_dev)

    def forward(u):
        n, g = unit(u)
        out = jnp.zeros((tok, 2 * CW), F32)
        for h in range(2):
            w = panel[n, :, 2 * h : 2 * h + 2].reshape(NX * 2 * ROWS, 2 * CW)
            out = out + jnp.dot(xp[g, h], w, preferred_element_type=F32)
        part[u] = out.reshape(2, half, 2 * CW).astype(BF)
        z1(u).start()

    def deltas(u):
        n, g = unit(u)
        z1(u).wait()
        total = part[u, r].astype(F32) + zin[u].astype(F32)
        gate, up = total[:, :CW], total[:, CW:]
        sig = jax.nn.sigmoid(gate)
        act = gate * sig
        hb[g, :, span(n, 1)] = (act * up).astype(BF)
        upstream = ctb[g, :, span(n, 1)].astype(F32)
        gd = (upstream * up * sig * (1.0 + gate * (1.0 - sig))).astype(BF)
        ud = (upstream * act).astype(BF)
        dl[u, r] = jnp.concatenate([gd, ud], axis=1)
        z2(u, r).start()

    def grads(u):
        n, g = unit(u)
        z2(u, 1 - r).wait_recv()
        z2(u, r).wait_send()
        new_tile = among(u, FIRST_OF_TILE)
        new_group = among(u, FIRST_OF_GROUP)
        last = among(u, LAST_OF_TILE)

        def dgrad(i, carry):
            w = panel[n, i].reshape(NX * ROWS, 2 * CW)
            v = lax.dot_general(
                dl[u].reshape(tok, 2 * CW), w, (((1,), (1,)), ((), ())), preferred_element_type=F32
            )
            sl = pl.ds(pl.multiple_of(i * NX * ROWS, NX * ROWS), NX * ROWS)

            @pl.when(new_group)
            def _():
                acc[g, :, sl] = v

            @pl.when(jnp.logical_not(new_group))
            def _():
                acc[g, :, sl] += v

            return carry

        lax.fori_loop(0, NX, dgrad, 0)
        for m, v in enumerate(LAST_OF_GROUP):
            pl.when(u == v)(functools.partial(dx0, m))

        def wgrad(i, carry):
            p = ring(x, 2 + i)
            v = jnp.dot(xt[g, p], dl[u].reshape(tok, 2 * CW), preferred_element_type=F32)

            @pl.when(new_tile)
            def _():
                gacc[n, p] = v

            @pl.when(jnp.logical_not(new_tile))
            def _():
                gacc[n, p] += v

            @pl.when(last)
            def _():
                gp[n, p] = gacc[n, p].reshape(NX, ROWS, 2 * CW).astype(BF)

            @pl.when(last & (i == 0))
            def _():
                for h in range(2):
                    rs(0, n, h).start()

            return carry

        lax.fori_loop(0, NX, wgrad, 0)

        @pl.when(last)
        def _():
            for h in range(2):
                rs(1, n, h).start()

    def rs(stage, n, i):
        p = ring(x, 2) if stage == 0 else ring(x, 1 - 2 * i)
        rows = pl.ds(2 * (1 - i if stage == 1 else i), 2)
        dst = rb0.at[n, i] if stage == 0 else rb1.at[n, i, rows]
        return remote(gp.at[n, p, rows], dst, rs_s.at[stage, i, n], rs_r.at[stage, i, n], x_dev(1 - 2 * i))

    def add(ref, *others):
        v = ref[...].astype(F32)
        for o in others:
            v = v + o[...].astype(F32)
        ref[...] = v.astype(BF)

    def rs1(n):
        for i in range(2):
            rs(0, n, i).wait()
            add(gp.at[n, ring(x, 1 - 2 * i), pl.ds(2 * i, 2)], rb0.at[n, i])
            rs(2, n, i).start()

    def ga(q, n, to, frm):
        return remote(gp.at[n, x, to], gr.at[frm, n], ga_s.at[q, n], ga_r.at[q, n], y_dev(OFF[q]))

    def rs2(n):
        for i in range(2):
            rs(1, n, i).wait()
            rs(2, n, i).wait()
        add(gp.at[n, x], rb1.at[n, 0], rb1.at[n, 1])
        for q in range(3):
            ga(q, n, ring(y, OFF[q]), y).start()
        gr[y, n] = gp[n, x, y]

    def rs3(n):
        for q in range(3):
            ga(q, n, y, ring(y, -OFF[q])).wait_recv()

        if n < NT - 1:
            for p in range(NX):
                at = slice((3 * p + (p + 1) // 2 + n) * CW, (3 * p + (p + 1) // 2 + n + 1) * CW)
                gg[0, :, at] = gr[p, n, :, :CW]
                ug[0, :, at] = gr[p, n, :, CW:]
        else:
            for p in range(2):
                v = (gr[2 * p, n].astype(F32) + gr[2 * p + 1, n].astype(F32)).astype(BF)
                at = slice((3 + 7 * p) * CW, (4 + 7 * p) * CW)
                gg[0, :, at] = v[:, :CW]
                ug[0, :, at] = v[:, CW:]

    def hd(q, g, frm):
        return remote(
            hb.at[g, :, 0 : 3 * CW], hid.at[:, span(first_tile(frm), 3)], hd_s.at[q], hd_r.at[q], y_dev(OFF[q])
        )

    def hd_shared(g, frm):
        return remote(
            hb.at[g, :, 3 * CW :], hid.at[:, span(shared_tile(frm), 1)], hd_s.at[3], hd_r.at[3], y_dev(2)
        )

    def hidden(q):
        hd(q, ring(y, OFF[q]), y).start()
        if q == 0:
            hd_shared(ring(y, 2), y).start()

    def hidden_own():
        hid[:, span(first_tile(y), 3)] = hb[y, :, 0 : 3 * CW]
        hid[:, span(shared_tile(y), 1)] = hb[y, :, 3 * CW :]

    def hidden_end():
        for q in range(3):
            hd(q, y, ring(y, -OFF[q])).wait_recv()
        hd_shared(y, ring(y, 2)).wait_recv()
        result(0).start()

    def d_sib(m):
        return remote(dxs.at[m], dxr.at[m], ds_s.at[m], ds_r.at[m], sib_dev)

    def d_side(q, s):
        b = ring(zl, s)
        return remote(dys.at[q, b], dyr.at[q, b], dy_s.at[q, s], dy_r.at[q, s], y_dev(OFF[q]))

    def d_line(s):
        return remote(dxz.at[s - 1], dxq.at[s - 1], dz_s.at[s - 1], dz_r.at[s - 1], z_dev(s))

    def group_at(m):
        return y if m == 0 else ring(y, OFF[m - 1])

    def d_own(s):
        b = ring(zl, s)
        return remote(dxs.at[0, b], dxr.at[0, b], do_s.at[s], do_r.at[s], sib_dev)

    def dx0(m):
        for s in (2, 1, 3, 0):
            b = ring(zl, s)
            dxs[m, b] = acc[group_at(m), :, feat(2 * b + 1 - k)].astype(BF)
            if m == 0:
                d_own(s).start()
        if m > 0:
            d_sib(m).start()

    def dx1(m):
        d_sib(m).wait()
        for s in (2, 1, 3, 0):
            b = ring(zl, s)
            dys[m - 1, b] = (acc[group_at(m), :, feat(2 * b + k)] + dxr[m, b].astype(F32)).astype(BF)
            d_side(m - 1, s).start()

    def dx_sum(b):
        v = acc[y, :, feat(2 * b + k)] + dxr[0, b].astype(F32)
        for q in range(3):
            v = v + dyr[q, b].astype(F32)
        return v

    def dx2():
        for s in (2, 1, 3):
            d_own(s).wait()
            for q in range(3):
                d_side(q, s).wait()
            dxz[s - 1] = dx_sum(ring(zl, s)).astype(BF)
            d_line(s).start()

    def dx3():
        d_own(0).wait()
        for q in range(3):
            d_side(q, 0).wait()
        v = dx_sum(zl)
        for s in (1, 2, 3):
            d_line(s).wait()
            v = v + dxq[s - 1].astype(F32)
        dx[...] = v.astype(BF)
        result(1).start()

    outs = ((hid, hid_hbm), (dx, dx_hbm), (gg, gg_hbm), (ug, ug_hbm))

    def result(n):
        return pltpu.make_async_copy(*outs[n], out_sem.at[n])

    own_x.wait()
    for s in (2, 1, 3):
        x_line(s, zl).start()
    pltpu.make_async_copy(wpk, wpk, in_sem.at[1]).wait()
    wa_start(0)
    wa_start(1)
    x_side(0, 0, y).start()
    wa_start(2)
    wa_start(3)
    wg1(0)
    x_arrive(1)
    wg2(0)
    wg1(1)
    x_arrive(3)
    x_arrive(2)
    x_sib(0, y, k).start()
    ct(0, ring(y, 2), y).start()
    ct_shared(ring(y, 2), y).start()
    for copy in own_cot:
        copy.wait()
    wg3(0)
    x_ready(0, y)

    def settle():
        for n in range(NT):
            for q in range(3):
                wa(q, n, ring(y, OFF[q]), y).wait_send()
            for i in range(2):
                wx(0, n, i, 0).wait_send()
                wx(1, n, i, -1 + 2 * i).wait_send()
            x_sib(n, y, k).wait_send()
            x_side(0, n, y).wait_send()
        for q in range(3):
            x_line(q + 1, zl).wait_send()
            ct(q, ring(y, OFF[q]), y).wait_send()
        ct_shared(ring(y, 2), y).wait_send()
        x_whole(1, y).wait_send()
        x_whole(2, y).wait_send()

    og = SD + SG

    def tick(t, carry):
        def on(at, fn, *args):
            pl.when(t == at)(functools.partial(fn, *args))

        def at(off, fn):
            u = t - off

            @pl.when((u >= 0) & (u < UNITS))
            def _():
                fn(u)

        on(SD + FIRST_OF_GROUP[2], ct_wait, 2)
        on(SD + FIRST_OF_GROUP[3], ct_wait, 1)
        on(1, deltas, 0)
        on(SD + FIRST_OF_GROUP[1], ct_wait, 0)
        pl.when((t > SD) & (t < UNITS + SD - 1))(lambda: deltas(t - SD))
        on(1, x_ready, 1, ring(y, 2))
        on(2, wg3, 1)
        on(3, wg3, 2)
        on(4, wg3, 3)
        on(FIRST_OF_GROUP[2], x_ready, 3, ring(y, 1))
        on(FIRST_OF_GROUP[3], x_ready, 2, ring(y, -1))
        at(0, forward)
        on(0, wg2, 1)
        on(0, wg1, 2)
        on(0, x_group, 0)
        on(0, x_rest)
        on(1, wg2, 2)
        on(1, wg1, 3)
        on(3, wg2, 3)
        on(FIRST_OF_GROUP[2] - 2, x_group, 2)
        on(FIRST_OF_GROUP[3] - 2, x_group, 1)
        for n, u in enumerate(LAST_OF_TILE):
            if u < UNITS - 1:
                on(og + u + 1, rs1, n)
        at(og, grads)
        on(UNITS + SD - 2, deltas, UNITS - 1)
        on(SD + LAST_OF_GROUP[0], hidden_own)
        for q in range(3):
            on(SD + LAST_OF_GROUP[q + 1], hidden, q)
        for m in range(1, 4):
            on(og + LAST_OF_GROUP[m] + 1, dx1, m)
        on(og + LAST_OF_GROUP[0] + 1, dx2)
        on(og + UNITS, rs1, ORDER[-1][0])
        for n, u in enumerate(LAST_OF_TILE):
            on(og + u + 3, rs3, n)
        for n, u in enumerate(LAST_OF_TILE):
            on(og + u + 2, rs2, n)
        on(UNITS - 1, settle)
        on(og + UNITS + 1, hidden_end)
        on(og + UNITS + 2, dx3)
        return carry

    lax.fori_loop(0, og + UNITS + 3, tick, 0)
    result(2).start()
    result(3).start()
    for q in range(3):
        for n in range(NT):
            ga(q, n, ring(y, OFF[q]), y).wait_send()
        hd(q, ring(y, OFF[q]), y).wait_send()
    hd_shared(ring(y, 2), y).wait_send()
    for n in range(4):
        result(n).wait()


def hand_on(*refs):
    ins, outs, held, in_sem, out_sem = refs[:4], refs[4:8], refs[8:12], refs[12], refs[13]
    reads = [pltpu.make_async_copy(a, b, in_sem.at[n]) for n, (a, b) in enumerate(zip(ins, held))]
    writes = [pltpu.make_async_copy(a, b, out_sem.at[n]) for n, (a, b) in enumerate(zip(held, outs))]
    for read in reads:
        read.start()
    for read, write in zip(reads, writes):
        read.wait()
        write.start()
    for write in writes:
        write.wait()


def local(inputs, gate_weight, up_weight, cotangent):
    tok, fb = inputs.shape
    _, rows, width = gate_weight.shape
    half = cotangent.shape[0]
    feats = rows * NX * NX
    vm, dma = pltpu.VMEM, pltpu.SemaphoreType.DMA
    any_spec = pl.BlockSpec(memory_space=pl.ANY)
    shapes = ((half, width), (tok, fb), (1, rows, width), (1, rows, width))
    out_shape = tuple(jax.ShapeDtypeStruct(shape, BF) for shape in shapes)
    results = pl.pallas_call(
        kernel,
        out_shape=out_shape,
        in_specs=[any_spec] * 4,
        out_specs=[any_spec] * 4,
        scratch_shapes=[
            *(vm(shape, BF) for shape in shapes),
            vm((width // CW, rows, 2 * CW), BF),
            vm((NT, NX, NX, rows, 2 * CW), BF),
            vm((NX, 2, tok, feats // 2), BF),
            vm((NX, NX, NX * rows, tok), BF),
            vm((NX, tok, feats), F32),
            vm((NT, NX, NX * rows, 2 * CW), F32),
            vm((NT, NX, NX, rows, 2 * CW), BF),
            vm((NT, 2, 2, rows, 2 * CW), BF),
            vm((NT, 2, NX, rows, 2 * CW), BF),
            vm((NX, NT, rows, 2 * CW), BF),
            vm((UNITS, 2, half, 2 * CW), BF),
            vm((UNITS, half, 2 * CW), BF),
            vm((UNITS, 2, half, 2 * CW), BF),
            vm((NX, half, NT * CW), BF),
            vm((NX, half, NT * CW), BF),
            vm((4, 4, tok, fb), BF),
            vm((4, 4, tok, fb), BF),
            vm((3, 4, tok, fb), BF),
            vm((3, 4, tok, fb), BF),
            vm((3, tok, fb), BF),
            vm((3, tok, fb), BF),
            dma((4,)),
            dma((NT,)),
            dma((4,)),
            *(dma((3, NT)) for _ in range(2)),
            *(dma((2, 2, NT)) for _ in range(2)),
            *(dma((3,)) for _ in range(2)),
            *(dma((3, 4)) for _ in range(2)),
            *(dma((4,)) for _ in range(2)),
            *(dma((4,)) for _ in range(2)),
            *(dma((2, UNITS)) for _ in range(2)),
            *(dma((3, 2, NT)) for _ in range(2)),
            *(dma((3, NT)) for _ in range(2)),
            *(dma((4,)) for _ in range(2)),
            *(dma((4,)) for _ in range(2)),
            *(dma((4,)) for _ in range(2)),
            *(dma((3, 4)) for _ in range(2)),
            *(dma((3,)) for _ in range(2)),
        ],
        compiler_params=pltpu.CompilerParams(
            collective_id=0, has_side_effects=True, vmem_limit_bytes=62 * 2**20
        ),
    )(inputs, gate_weight, up_weight, cotangent)
    return pl.pallas_call(
        hand_on,
        out_shape=out_shape,
        in_specs=[any_spec] * 4,
        out_specs=[any_spec] * 4,
        scratch_shapes=[*(vm(shape, BF) for shape in shapes), dma((4,)), dma((4,))],
    )(*results)


def solution(mesh):
    return jax.shard_map(
        local,
        mesh=mesh,
        in_specs=(
            P("depth", ("row", "col")),
            P("row", "depth", "col"),
            P("row", "depth", "col"),
            P(("depth", "row"), "col"),
        ),
        out_specs=(
            P(("depth", "row"), "col"),
            P("depth", ("row", "col")),
            P("row", "depth", "col"),
            P("row", "depth", "col"),
        ),
        check_vma=False,
    )
```

```python
import functools

import jax
import jax.numpy as jnp
from jax import lax
from jax.experimental import pallas as pl
from jax.experimental.pallas import tpu as pltpu
from jax.sharding import PartitionSpec as P

MESH = pl.DeviceIdType.MESH
BF = jnp.bfloat16
F32 = jnp.float32
NX = 4
ROWS = 128
CW = 128
NT = 4
ORDER = (
    (0, 0), (0, 1), (1, 1), (2, 1), (3, 1), (3, 0), (0, 2), (0, 3), (1, 2), (2, 2),
    (1, 3), (2, 3), (1, 0), (2, 0),
)
UNITS = len(ORDER)
TILES = sum(n << 2 * u for u, (n, _) in enumerate(ORDER))
SHIFTS = sum((0, 2, 1, 3)[m] << 2 * u for u, (_, m) in enumerate(ORDER))
FIRST_OF_TILE = [min(u for u, (n, _) in enumerate(ORDER) if n == i) for i in range(NT)]
LAST_OF_TILE = [max(u for u, (n, _) in enumerate(ORDER) if n == i) for i in range(NT)]
FIRST_OF_GROUP = [min(u for u, (_, m) in enumerate(ORDER) if m == i) for i in range(4)]
LAST_OF_GROUP = [max(u for u, (_, m) in enumerate(ORDER) if m == i) for i in range(4)]
OFF = (2, 1, -1)
SD = 2
SG = 1


def kernel(
    x_hbm, gw_hbm, uw_hbm, cot_hbm, hid_hbm, dx_hbm, gg_hbm, ug_hbm,
    hid, dx, gg, ug, wpk, panel, xp, xt, acc, gacc, gp, rb0, rb1, gr, part, zin, dl, ctb, hb,
    dxs, dxr, dys, dyr, dxz, dxq,
    in_sem, own_sem, out_sem, wa_s, wa_r, wx_s, wx_r, xz_s, xz_r, xy_s, xy_r, xs_s, xs_r, ct_s, ct_r,
    z_s, z_r, rs_s, rs_r, ga_s, ga_r, hd_s, hd_r, ds_s, ds_r, do_s, do_r, dy_s, dy_r, dz_s, dz_r,
):
    d, r, c = lax.axis_index("depth"), lax.axis_index("row"), lax.axis_index("col")
    x, y = lax.div(d, NX), lax.rem(d, NX)
    zl, k = lax.div(c, 2), lax.rem(c, 2)
    tok, fb = dx.shape
    half = tok // 2

    def ring(p, s):
        return lax.rem(p + s + NX, NX)

    def x_dev(s):
        return {"depth": ring(x, s) * NX + y}

    def y_dev(s):
        return {"depth": x * NX + ring(y, s)}

    row_dev = {"row": 1 - r}
    sib_dev = {"col": c + 1 - 2 * k}

    def z_dev(s):
        return {"col": ring(zl, s) * 2 + k}

    def remote(src, dst, ssem, rsem, dev):
        return pltpu.make_async_remote_copy(
            src_ref=src, dst_ref=dst, send_sem=ssem, recv_sem=rsem, device_id=dev, device_id_type=MESH
        )

    def span(start, n):
        return pl.ds(pl.multiple_of(start * CW, CW), n * CW)

    def first_tile(q):
        return 3 * q + lax.div(q + 1, 2)

    def shared_tile(q):
        return 3 + 7 * lax.div(q, 2)

    def tile_of(q, n):
        return first_tile(q) + n if n < NT - 1 else shared_tile(q)

    def feat(b):
        return pl.ds(pl.multiple_of(b * fb, fb), fb)

    def own(n, s):
        src = (gw_hbm, uw_hbm)[s].at[0, :, span(n, 1)]
        return pltpu.make_async_copy(src, wpk.at[n, :, s * CW : (s + 1) * CW], in_sem.at[1])

    def own_start(n, carry):
        for s in range(2):
            own(n, s).start()
        return carry

    def own_tile(n):
        return pltpu.make_async_copy(wpk.at[tile_of(y, n)], panel.at[n, x, y], own_sem.at[n])

    own_x = pltpu.make_async_copy(x_hbm, xp.at[y, k, :, feat(zl)], in_sem.at[0])
    own_cot = (
        pltpu.make_async_copy(cot_hbm.at[:, span(first_tile(y), 3)], ctb.at[y, :, 0 : 3 * CW], in_sem.at[2]),
        pltpu.make_async_copy(cot_hbm.at[:, span(shared_tile(y), 1)], ctb.at[y, :, 3 * CW :], in_sem.at[3]),
    )
    own_x.start()
    lax.fori_loop(0, wpk.shape[0], own_start, 0)
    for copy in own_cot:
        copy.start()

    partners = [x_dev(1), x_dev(-1), y_dev(1), y_dev(-1), y_dev(2), row_dev, sib_dev, z_dev(1), z_dev(2), z_dev(3)]
    barrier = pltpu.get_barrier_semaphore()
    for dev in partners:
        pl.semaphore_signal(barrier, inc=1, device_id=dev, device_id_type=MESH)
    pl.semaphore_wait(barrier, len(partners))

    def wa(q, n, to, frm):
        return remote(wpk.at[tile_of(to, n)], panel.at[n, x, frm], wa_s.at[q, n], wa_r.at[q, n], y_dev(OFF[q]))

    def wa_start(n):
        own_tile(n).start()
        for q in range(3):
            wa(q, n, ring(y, OFF[q]), y).start()

    def wx(stage, n, i, shift):
        p = ring(x, shift)
        src = panel.at[n, p] if stage == 0 else panel.at[n, p, pl.ds(2 * i, 2)]
        return remote(src, src, wx_s.at[stage, i, n], wx_r.at[stage, i, n], x_dev(1 - 2 * i))

    def wg1(n):
        own_tile(n).wait()
        for q in range(3):
            wa(q, n, y, ring(y, -OFF[q])).wait_recv()
        for i in range(2):
            wx(0, n, i, 0).start()

    def wg2(n):
        for i in range(2):
            wx(0, n, i, -1 + 2 * i).wait_recv()
            wx(1, n, i, -1 + 2 * i).start()

    def wg3(n):
        for i in range(2):
            wx(1, n, i, 2).wait_recv()

    def x_line(s, b):
        blk = xp.at[y, k, :, feat(b)]
        return remote(blk, blk, xz_s.at[s - 1], xz_r.at[s - 1], z_dev(s))

    def x_side(q, n, g):
        blk = xp.at[g, k, :, feat(ring(zl, -n))]
        return remote(blk, blk, xy_s.at[q, n], xy_r.at[q, n], y_dev(OFF[q]))

    def x_sib(n, g, h):
        blk = xp.at[g, h]
        return remote(blk, blk, xs_s.at[n], xs_r.at[n], sib_dev)

    def x_whole(q, g):
        blk = xp.at[g, k]
        return remote(blk, blk, xy_s.at[q, 0], xy_r.at[q, 0], y_dev(OFF[q]))

    def x_arrive(s):
        x_line(s, ring(zl, -s)).wait_recv()
        x_side(0, s, y).start()

    def x_rest():
        for q in (2, 1):
            x_whole(q, y).start()
            ct(q, ring(y, OFF[q]), y).start()

    def x_from(q):
        return ring(y, -OFF[q])

    def x_group(q):
        g = x_from(q)
        if q == 0:
            for n in range(4):
                x_side(q, n, g).wait_recv()
        else:
            x_whole(q, g).wait_recv()
        x_sib(q + 1, g, k).start()

    def x_ready(n, g):
        x_sib(n, g, 1 - k).wait_recv()
        for i in range(NX):
            w = slice(i * fb, (i + 1) * fb)
            xt[g, i] = jnp.concatenate([jnp.transpose(xp[g, 0, :, w]), jnp.transpose(xp[g, 1, :, w])], axis=0)

    def ct(q, to, frm):
        return remote(
            cot_hbm.at[:, span(first_tile(to), 3)], ctb.at[frm, :, 0 : 3 * CW], ct_s.at[q], ct_r.at[q], y_dev(OFF[q])
        )

    def ct_shared(to, frm):
        return remote(
            cot_hbm.at[:, span(shared_tile(to), 1)], ctb.at[frm, :, 3 * CW :], ct_s.at[3], ct_r.at[3], y_dev(2)
        )

    def ct_wait(q):
        if q == 0:
            ct_shared(y, ring(y, 2)).wait_recv()
        ct(q, y, ring(y, -OFF[q])).wait_recv()

    def unit(u):
        n = lax.rem(lax.shift_right_logical(jnp.int32(TILES), 2 * u), 4)
        shift = lax.rem(lax.shift_right_logical(jnp.int32(SHIFTS), 2 * u), 4)
        return n, lax.rem(y + shift, NX)

    def among(u, units):
        hit = u == units[0]
        for v in units[1:]:
            hit = hit | (u == v)
        return hit

    def z1(u):
        return remote(part.at[u, 1 - r], zin.at[u], z_s.at[0, u], z_r.at[0, u], row_dev)

    def z2(u, h):
        blk = dl.at[u, h]
        return remote(blk, blk, z_s.at[1, u], z_r.at[1, u], row_dev)

    def forward(u):
        n, g = unit(u)
        out = jnp.zeros((tok, 2 * CW), F32)
        for h in range(2):
            w = panel[n, :, 2 * h : 2 * h + 2].reshape(NX * 2 * ROWS, 2 * CW)
            out = out + jnp.dot(xp[g, h], w, preferred_element_type=F32)
        part[u] = out.reshape(2, half, 2 * CW).astype(BF)
        z1(u).start()

    def deltas(u):
        n, g = unit(u)
        z1(u).wait()
        total = part[u, r].astype(F32) + zin[u].astype(F32)
        gate, up = total[:, :CW], total[:, CW:]
        sig = jax.nn.sigmoid(gate)
        act = gate * sig
        hb[g, :, span(n, 1)] = (act * up).astype(BF)
        upstream = ctb[g, :, span(n, 1)].astype(F32)
        gd = (upstream * up * sig * (1.0 + gate * (1.0 - sig))).astype(BF)
        ud = (upstream * act).astype(BF)
        dl[u, r] = jnp.concatenate([gd, ud], axis=1)
        z2(u, r).start()

    def grads(u):
        n, g = unit(u)
        z2(u, 1 - r).wait_recv()
        z2(u, r).wait_send()
        new_tile = among(u, FIRST_OF_TILE)
        new_group = among(u, FIRST_OF_GROUP)
        last = among(u, LAST_OF_TILE)

        def dgrad(i, carry):
            w = panel[n, i].reshape(NX * ROWS, 2 * CW)
            v = lax.dot_general(
                dl[u].reshape(tok, 2 * CW), w, (((1,), (1,)), ((), ())), preferred_element_type=F32
            )
            sl = pl.ds(pl.multiple_of(i * NX * ROWS, NX * ROWS), NX * ROWS)

            @pl.when(new_group)
            def _():
                acc[g, :, sl] = v

            @pl.when(jnp.logical_not(new_group))
            def _():
                acc[g, :, sl] += v

            return carry

        lax.fori_loop(0, NX, dgrad, 0)
        for m, v in enumerate(LAST_OF_GROUP):
            pl.when(u == v)(functools.partial(dx0, m))

        def wgrad(i, carry):
            p = ring(x, 2 + i)
            v = jnp.dot(xt[g, p], dl[u].reshape(tok, 2 * CW), preferred_element_type=F32)

            @pl.when(new_tile)
            def _():
                gacc[n, p] = v

            @pl.when(jnp.logical_not(new_tile))
            def _():
                gacc[n, p] += v

            @pl.when(last)
            def _():
                gp[n, p] = gacc[n, p].reshape(NX, ROWS, 2 * CW).astype(BF)

            @pl.when(last & (i == 0))
            def _():
                for h in range(2):
                    rs(0, n, h).start()

            return carry

        lax.fori_loop(0, NX, wgrad, 0)

        @pl.when(last)
        def _():
            for h in range(2):
                rs(1, n, h).start()

    def rs(stage, n, i):
        p = ring(x, 2) if stage == 0 else ring(x, 1 - 2 * i)
        rows = pl.ds(2 * (1 - i if stage == 1 else i), 2)
        dst = rb0.at[n, i] if stage == 0 else rb1.at[n, i, rows]
        return remote(gp.at[n, p, rows], dst, rs_s.at[stage, i, n], rs_r.at[stage, i, n], x_dev(1 - 2 * i))

    def add(ref, *others):
        v = ref[...].astype(F32)
        for o in others:
            v = v + o[...].astype(F32)
        ref[...] = v.astype(BF)

    def rs1(n):
        for i in range(2):
            rs(0, n, i).wait()
            add(gp.at[n, ring(x, 1 - 2 * i), pl.ds(2 * i, 2)], rb0.at[n, i])
            rs(2, n, i).start()

    def ga(q, n, to, frm):
        return remote(gp.at[n, x, to], gr.at[frm, n], ga_s.at[q, n], ga_r.at[q, n], y_dev(OFF[q]))

    def rs2(n):
        for i in range(2):
            rs(1, n, i).wait()
            rs(2, n, i).wait()
        add(gp.at[n, x], rb1.at[n, 0], rb1.at[n, 1])
        for q in range(3):
            ga(q, n, ring(y, OFF[q]), y).start()
        gr[y, n] = gp[n, x, y]

    def rs3(n):
        for q in range(3):
            ga(q, n, y, ring(y, -OFF[q])).wait_recv()

        if n < NT - 1:
            for p in range(NX):
                at = slice((3 * p + (p + 1) // 2 + n) * CW, (3 * p + (p + 1) // 2 + n + 1) * CW)
                gg[0, :, at] = gr[p, n, :, :CW]
                ug[0, :, at] = gr[p, n, :, CW:]
        else:
            for p in range(2):
                v = (gr[2 * p, n].astype(F32) + gr[2 * p + 1, n].astype(F32)).astype(BF)
                at = slice((3 + 7 * p) * CW, (4 + 7 * p) * CW)
                gg[0, :, at] = v[:, :CW]
                ug[0, :, at] = v[:, CW:]

    def hd(q, g, frm):
        return remote(
            hb.at[g, :, 0 : 3 * CW], hid.at[:, span(first_tile(frm), 3)], hd_s.at[q], hd_r.at[q], y_dev(OFF[q])
        )

    def hd_shared(g, frm):
        return remote(
            hb.at[g, :, 3 * CW :], hid.at[:, span(shared_tile(frm), 1)], hd_s.at[3], hd_r.at[3], y_dev(2)
        )

    def hidden(q):
        hd(q, ring(y, OFF[q]), y).start()
        if q == 0:
            hd_shared(ring(y, 2), y).start()

    def hidden_own():
        hid[:, span(first_tile(y), 3)] = hb[y, :, 0 : 3 * CW]
        hid[:, span(shared_tile(y), 1)] = hb[y, :, 3 * CW :]

    def hidden_end():
        for q in range(3):
            hd(q, y, ring(y, -OFF[q])).wait_recv()
        hd_shared(y, ring(y, 2)).wait_recv()
        result(0).start()

    def d_sib(m):
        return remote(dxs.at[m], dxr.at[m], ds_s.at[m], ds_r.at[m], sib_dev)

    def d_side(q, s):
        b = ring(zl, s)
        return remote(dys.at[q, b], dyr.at[q, b], dy_s.at[q, s], dy_r.at[q, s], y_dev(OFF[q]))

    def d_line(s):
        return remote(dxz.at[s - 1], dxq.at[s - 1], dz_s.at[s - 1], dz_r.at[s - 1], z_dev(s))

    def group_at(m):
        return y if m == 0 else ring(y, OFF[m - 1])

    def d_own(s):
        b = ring(zl, s)
        return remote(dxs.at[0, b], dxr.at[0, b], do_s.at[s], do_r.at[s], sib_dev)

    def dx0(m):
        for s in (2, 1, 3, 0):
            b = ring(zl, s)
            dxs[m, b] = acc[group_at(m), :, feat(2 * b + 1 - k)].astype(BF)
            if m == 0:
                d_own(s).start()
        if m > 0:
            d_sib(m).start()

    def dx1(m):
        d_sib(m).wait()
        for s in (2, 1, 3, 0):
            b = ring(zl, s)
            dys[m - 1, b] = (acc[group_at(m), :, feat(2 * b + k)] + dxr[m, b].astype(F32)).astype(BF)
            d_side(m - 1, s).start()

    def dx_sum(b):
        v = acc[y, :, feat(2 * b + k)] + dxr[0, b].astype(F32)
        for q in range(3):
            v = v + dyr[q, b].astype(F32)
        return v

    def dx2():
        for s in (2, 1, 3):
            d_own(s).wait()
            for q in range(3):
                d_side(q, s).wait()
            dxz[s - 1] = dx_sum(ring(zl, s)).astype(BF)
            d_line(s).start()

    def dx3():
        d_own(0).wait()
        for q in range(3):
            d_side(q, 0).wait()
        v = dx_sum(zl)
        for s in (1, 2, 3):
            d_line(s).wait()
            v = v + dxq[s - 1].astype(F32)
        dx[...] = v.astype(BF)
        result(1).start()

    outs = ((hid, hid_hbm), (dx, dx_hbm), (gg, gg_hbm), (ug, ug_hbm))

    def result(n):
        return pltpu.make_async_copy(*outs[n], out_sem.at[n])

    own_x.wait()
    for s in (2, 1, 3):
        x_line(s, zl).start()
    pltpu.make_async_copy(wpk, wpk, in_sem.at[1]).wait()
    wa_start(0)
    wa_start(1)
    x_side(0, 0, y).start()
    wa_start(2)
    wa_start(3)
    wg1(0)
    x_arrive(1)
    wg2(0)
    wg1(1)
    x_arrive(3)
    x_arrive(2)
    x_sib(0, y, k).start()
    ct(0, ring(y, 2), y).start()
    ct_shared(ring(y, 2), y).start()
    for copy in own_cot:
        copy.wait()
    wg3(0)
    x_ready(0, y)

    def settle():
        for n in range(NT):
            for q in range(3):
                wa(q, n, ring(y, OFF[q]), y).wait_send()
            for i in range(2):
                wx(0, n, i, 0).wait_send()
                wx(1, n, i, -1 + 2 * i).wait_send()
            x_sib(n, y, k).wait_send()
            x_side(0, n, y).wait_send()
        for q in range(3):
            x_line(q + 1, zl).wait_send()
            ct(q, ring(y, OFF[q]), y).wait_send()
        ct_shared(ring(y, 2), y).wait_send()
        x_whole(1, y).wait_send()
        x_whole(2, y).wait_send()

    og = SD + SG

    def tick(t, carry):
        def on(at, fn, *args):
            pl.when(t == at)(functools.partial(fn, *args))

        def at(off, fn):
            u = t - off

            @pl.when((u >= 0) & (u < UNITS))
            def _():
                fn(u)

        on(SD + FIRST_OF_GROUP[2], ct_wait, 2)
        on(SD + FIRST_OF_GROUP[3], ct_wait, 1)
        on(1, deltas, 0)
        on(SD + FIRST_OF_GROUP[1], ct_wait, 0)
        pl.when((t > SD) & (t < UNITS + SD - 1))(lambda: deltas(t - SD))
        on(1, x_ready, 1, ring(y, 2))
        on(2, wg3, 1)
        on(3, wg3, 2)
        on(4, wg3, 3)
        on(FIRST_OF_GROUP[2], x_ready, 3, ring(y, 1))
        on(FIRST_OF_GROUP[3], x_ready, 2, ring(y, -1))
        at(0, forward)
        on(0, wg2, 1)
        on(0, wg1, 2)
        on(0, x_group, 0)
        on(0, x_rest)
        on(1, wg2, 2)
        on(1, wg1, 3)
        on(3, wg2, 3)
        on(FIRST_OF_GROUP[2] - 2, x_group, 2)
        on(FIRST_OF_GROUP[3] - 2, x_group, 1)
        for n, u in enumerate(LAST_OF_TILE):
            if u < UNITS - 1:
                on(og + u + 1, rs1, n)
        at(og, grads)
        on(UNITS + SD - 2, deltas, UNITS - 1)
        on(SD + LAST_OF_GROUP[0], hidden_own)
        for q in range(3):
            on(SD + LAST_OF_GROUP[q + 1], hidden, q)
        for m in range(1, 4):
            on(og + LAST_OF_GROUP[m] + 1, dx1, m)
        on(og + LAST_OF_GROUP[0] + 1, dx2)
        on(og + UNITS, rs1, ORDER[-1][0])
        for n, u in enumerate(LAST_OF_TILE):
            on(og + u + 3, rs3, n)
        for n, u in enumerate(LAST_OF_TILE):
            on(og + u + 2, rs2, n)
        on(UNITS - 1, settle)
        on(og + UNITS + 1, hidden_end)
        on(og + UNITS + 2, dx3)
        return carry

    lax.fori_loop(0, og + UNITS + 3, tick, 0)
    result(2).start()
    result(3).start()
    for q in range(3):
        for n in range(NT):
            ga(q, n, ring(y, OFF[q]), y).wait_send()
        hd(q, ring(y, OFF[q]), y).wait_send()
    hd_shared(ring(y, 2), y).wait_send()
    for n in range(4):
        result(n).wait()


def hand_on(*refs):
    ins, outs, held, in_sem, out_sem = refs[:4], refs[4:8], refs[8:12], refs[12], refs[13]
    reads = [pltpu.make_async_copy(a, b, in_sem.at[n]) for n, (a, b) in enumerate(zip(ins, held))]
    writes = [pltpu.make_async_copy(a, b, out_sem.at[n]) for n, (a, b) in enumerate(zip(held, outs))]
    for read in reads:
        read.start()
    for read, write in zip(reads, writes):
        read.wait()
        write.start()
    for write in writes:
        write.wait()


def local(inputs, gate_weight, up_weight, cotangent):
    tok, fb = inputs.shape
    _, rows, width = gate_weight.shape
    half = cotangent.shape[0]
    feats = rows * NX * NX
    vm, dma = pltpu.VMEM, pltpu.SemaphoreType.DMA
    any_spec = pl.BlockSpec(memory_space=pl.ANY)
    shapes = ((half, width), (tok, fb), (1, rows, width), (1, rows, width))
    out_shape = tuple(jax.ShapeDtypeStruct(shape, BF) for shape in shapes)
    results = pl.pallas_call(
        kernel,
        out_shape=out_shape,
        in_specs=[any_spec] * 4,
        out_specs=[any_spec] * 4,
        scratch_shapes=[
            *(vm(shape, BF) for shape in shapes),
            vm((width // CW, rows, 2 * CW), BF),
            vm((NT, NX, NX, rows, 2 * CW), BF),
            vm((NX, 2, tok, feats // 2), BF),
            vm((NX, NX, NX * rows, tok), BF),
            vm((NX, tok, feats), F32),
            vm((NT, NX, NX * rows, 2 * CW), F32),
            vm((NT, NX, NX, rows, 2 * CW), BF),
            vm((NT, 2, 2, rows, 2 * CW), BF),
            vm((NT, 2, NX, rows, 2 * CW), BF),
            vm((NX, NT, rows, 2 * CW), BF),
            vm((UNITS, 2, half, 2 * CW), BF),
            vm((UNITS, half, 2 * CW), BF),
            vm((UNITS, 2, half, 2 * CW), BF),
            vm((NX, half, NT * CW), BF),
            vm((NX, half, NT * CW), BF),
            vm((4, 4, tok, fb), BF),
            vm((4, 4, tok, fb), BF),
            vm((3, 4, tok, fb), BF),
            vm((3, 4, tok, fb), BF),
            vm((3, tok, fb), BF),
            vm((3, tok, fb), BF),
            dma((4,)),
            dma((NT,)),
            dma((4,)),
            *(dma((3, NT)) for _ in range(2)),
            *(dma((2, 2, NT)) for _ in range(2)),
            *(dma((3,)) for _ in range(2)),
            *(dma((3, 4)) for _ in range(2)),
            *(dma((4,)) for _ in range(2)),
            *(dma((4,)) for _ in range(2)),
            *(dma((2, UNITS)) for _ in range(2)),
            *(dma((3, 2, NT)) for _ in range(2)),
            *(dma((3, NT)) for _ in range(2)),
            *(dma((4,)) for _ in range(2)),
            *(dma((4,)) for _ in range(2)),
            *(dma((4,)) for _ in range(2)),
            *(dma((3, 4)) for _ in range(2)),
            *(dma((3,)) for _ in range(2)),
        ],
        compiler_params=pltpu.CompilerParams(
            collective_id=0, has_side_effects=True, vmem_limit_bytes=62 * 2**20
        ),
    )(inputs, gate_weight, up_weight, cotangent)
    return pl.pallas_call(
        hand_on,
        out_shape=out_shape,
        in_specs=[any_spec] * 4,
        out_specs=[any_spec] * 4,
        scratch_shapes=[*(vm(shape, BF) for shape in shapes), dma((4,)), dma((4,))],
    )(*results)


def solution(mesh):
    return jax.shard_map(
        local,
        mesh=mesh,
        in_specs=(
            P("depth", ("row", "col")),
            P("row", "depth", "col"),
            P("row", "depth", "col"),
            P(("depth", "row"), "col"),
        ),
        out_specs=(
            P(("depth", "row"), "col"),
            P("depth", ("row", "col")),
            P("row", "depth", "col"),
            P("row", "depth", "col"),
        ),
        check_vma=False,
    )
```
